512 devices in a mesh: ctx: 64 (over y_hi, z, core), head: 8 (over x, y_lo).
Axes of the slice: x: 4, y: 8 (y_hi: 4, y_lo: 2; y = y_hi * 2 + y_lo), z: 8, core: 2. Of those that a mesh axis runs over, the one named last changes fastest.
Arguments:
- queries: bfloat16 [8192, 6144], P('ctx', 'head'), may hold values from -320 to 320
- latent: bfloat16 [8192, 576], P('ctx'), may hold values from -6 to 6
- w_key: bfloat16 [512, 4096], P(None, 'head'), may hold values from -0.25 to 0.25
- w_value: bfloat16 [512, 4096], P(None, 'head'), may hold values from -0.25 to 0.25
- grad_out: bfloat16 [8192, 4096], P('ctx', 'head'), may hold values from -6 to 6
- segment_ids: int32 [8192], replicated, may hold values from 0 to 31, never falling along the last dimension, each value on 1 to 512 neighbouring positions
Outputs:
- attn_out: bfloat16 [8192, 4096], P('ctx', 'head')
- grad_queries: bfloat16 [8192, 6144], P('ctx', 'head')
- grad_latent: bfloat16 [8192, 576], P('ctx')
- grad_w_key: bfloat16 [512, 4096], P(None, 'head')
- grad_w_value: bfloat16 [512, 4096], P(None, 'head')
The draws below stay inside these ranges and needn't reach their ends.
Inputs may be any that keep to these rules, and one draw needn't show every extreme that they name: `segment_ids`: document ids never fall along the sequence; each document has at most 512 tokens and one has exactly 512.
All inputs are finite; a program needn't handle non-finite values.
Results may differ from the reference program's by a relative error of at most 0.03.
Values may be sent and summed in bfloat16 or wider, within the bound.
A program may use at most 64 MiB of HBM per device.

```python
import math
import jax
import jax.numpy as jnp
import numpy as np
from jax import lax

LAT = 512
ROPE = 64
NOPE = 128
VDIM = 128
TOK_DEV = 128
PREV = 4
HEADS = 32
TOKENS = 8192
DOC_MAX = 512
DOCS = 32
N_CTX = 64


def rope_parts(key):
    rope_base = jax.random.normal(jax.random.fold_in(key, 101), (TOKENS, ROPE), jnp.float32)
    rope_jitter = jax.random.normal(jax.random.fold_in(key, 102), (TOKENS, ROPE), jnp.float32)
    return (jnp.clip(rope_base, -5.0, 5.0), jnp.clip(rope_jitter, -5.0, 5.0))


def draw_latent(key, part):
    rope_base, rope_jitter = rope_parts(key)
    key = jax.random.fold_in(key, 1)
    content = jnp.clip(jax.random.normal(key, (TOKENS, LAT), jnp.float32), -6.0, 6.0)
    before_marked = ((jnp.arange(TOKENS) + 1) % 61 == 7)[:, None]
    following = jnp.roll(rope_base, -1, axis=0)
    rope_part = jnp.where(before_marked, following + 0.06 * rope_jitter, rope_base)
    return jnp.concatenate([content, rope_part], 1).astype(jnp.bfloat16)


def draw_queries(key, part):
    key = jax.random.fold_in(key, 2)
    values_drawn = jnp.clip(jax.random.normal(key, (TOKENS, HEADS, NOPE + ROPE), jnp.float32), -6.0, 6.0)
    return jnp.clip(values_drawn, -320.0, 320.0).reshape(TOKENS, HEADS * (NOPE + ROPE)).astype(jnp.bfloat16)


def level_of(own_key, extent, split, smallest, top_value):
    gain, own = 1.0, jax.random.fold_in(own_key, 6)
    for position, shards_of in split:
        heights = jnp.exp(jax.random.uniform(jax.random.fold_in(own, position), (shards_of,), jnp.float32, smallest / len(split), top_value / len(split)))
        gain = gain * jnp.repeat(heights, extent[position] // shards_of).reshape([-1 if axis == position else 1 for axis in range(len(extent))])
    return gain


def length_profile(count, total, reach, lean):
    portions = [(1 << 20) // math.isqrt(grade ** lean) + 1 for grade in range(2, count + 1)]
    rest, counts = total - reach - (count - 1), [1] * (count - 1)
    while rest > 0:
        movable = [i for i in range(count - 1) if counts[i] < reach]
        whole, budget = sum([portions[i] for i in movable]), rest
        for i in movable:
            more = min(reach - counts[i], max(1, budget * portions[i] // whole), rest)
            counts[i] = counts[i] + more
            rest = rest - more
    return np.array([reach] + counts)


def uneven(rng, number_of, total, reach, skew):
    if number_of == 2:
        one = jax.random.randint(rng, (), max(1, total - reach), min(reach, total - 1) + 1)
        return jnp.stack([one, total - one])
    sizes = jnp.asarray(length_profile(number_of, total, reach, skew), jnp.int32)
    couples = (number_of - 1) // 2
    source_of, receiver = sizes[1:1 + 2 * couples:2], sizes[2:2 + 2 * couples:2]
    room = jnp.minimum(source_of - 1, reach - receiver)
    shifted = jax.random.randint(jax.random.fold_in(rng, 1), (couples,), 0, 1 << 20) % (room + 1)
    sizes = sizes.at[1:1 + 2 * couples:2].set(source_of - shifted).at[2:2 + 2 * couples:2].set(receiver + shifted)
    return sizes[jax.random.permutation(jax.random.fold_in(rng, 2), number_of)]


def bell_draw(stream_key, dims, deviation, reach, cuts=(), kind=jnp.bfloat16):
    result = jax.random.normal(stream_key, dims, jnp.float32) * deviation
    if len(cuts) > 0:
        result = level_of(stream_key, dims, cuts, -0.22, 0.18) * result
    return jnp.clip(result, min=-reach, max=reach).astype(kind)


def setup_inputs(seed: int = 0) -> dict:
    streams_of = jax.random.split(jax.random.key(seed), 7)
    return {
        "queries": draw_queries(jax.random.fold_in(streams_of[6], 71), 0),
        "latent": draw_latent(jax.random.fold_in(streams_of[6], 71), 0),
        "w_key": bell_draw(streams_of[2], (LAT, HEADS * NOPE), LAT ** -0.5, 0.25, ((1, 8),)),
        "w_value": bell_draw(streams_of[3], (LAT, HEADS * VDIM), LAT ** -0.5, 0.25, ((1, 8),)),
        "grad_out": bell_draw(streams_of[4], (TOKENS, HEADS * VDIM), 1.0, 6.0, ((0, 64), (1, 8))),
        "segment_ids": jnp.searchsorted(jnp.cumsum(uneven(streams_of[5], DOCS, TOKENS, DOC_MAX, 0)), jnp.arange(TOKENS), side="right").astype(jnp.int32),
    }


def rounded(array):
    return lax.optimization_barrier(array.astype(jnp.bfloat16)).astype(jnp.float32)

def reference(queries, latent, w_key, w_value, grad_out, segment_ids):
    head_count = w_key.shape[1] // NOPE
    window = (PREV + 1) * TOK_DEV
    margin = PREV * TOK_DEV
    scale_factor = 1.0 / math.sqrt(NOPE + ROPE)
    latent_nope = latent[:, :LAT]
    latent_rope = latent[:, LAT:]
    keys_all = jnp.dot(latent_nope, w_key, preferred_element_type=jnp.float32).astype(jnp.bfloat16)
    values_all = jnp.dot(latent_nope, w_value, preferred_element_type=jnp.float32).astype(jnp.bfloat16)
    keys_padded = jnp.concatenate([jnp.zeros((margin, keys_all.shape[1]), jnp.bfloat16), keys_all], 0)
    values_padded = jnp.concatenate([jnp.zeros((margin, values_all.shape[1]), jnp.bfloat16), values_all], 0)
    rope_padded = jnp.concatenate([jnp.zeros((margin, ROPE), jnp.bfloat16), latent_rope], 0)
    segment_padded = jnp.concatenate([jnp.full((margin,), -1, jnp.int32), segment_ids.astype(jnp.int32)], 0)

    def one_block(sums, block_index):
        grad_keys, grad_values, grad_rope = sums
        row_start = (block_index * TOK_DEV).astype(jnp.int32)
        query_all = lax.dynamic_slice_in_dim(queries, row_start, TOK_DEV, 0).reshape(TOK_DEV, head_count, NOPE + ROPE).astype(jnp.float32)
        query_nope = query_all[:, :, :NOPE]
        query_rope = query_all[:, :, NOPE:]
        upstream = lax.dynamic_slice_in_dim(grad_out, row_start, TOK_DEV, 0).reshape(TOK_DEV, head_count, VDIM).astype(jnp.float32)
        key_nope = lax.dynamic_slice_in_dim(keys_padded, row_start, window, 0).reshape(window, head_count, NOPE).astype(jnp.float32)
        key_rope = lax.dynamic_slice_in_dim(rope_padded, row_start, window, 0).astype(jnp.float32)
        value_block = lax.dynamic_slice_in_dim(values_padded, row_start, window, 0).reshape(window, head_count, VDIM).astype(jnp.float32)
        query_segment = lax.dynamic_slice_in_dim(segment_ids.astype(jnp.int32), row_start, TOK_DEV, 0)
        key_segment = lax.dynamic_slice_in_dim(segment_padded, row_start, window, 0)
        query_pos = row_start + jnp.arange(TOK_DEV, dtype=jnp.int32)
        key_pos = row_start - margin + jnp.arange(window, dtype=jnp.int32)
        allowed = (key_pos[None, :] <= query_pos[:, None]) & (key_pos[None, :] >= 0) & (key_segment[None, :] == query_segment[:, None])
        scores = scale_factor * (jnp.einsum('thd,whd->htw', query_nope, key_nope) + jnp.einsum('thd,wd->htw', query_rope, key_rope))
        masked = jnp.where(allowed[None], scores, -jnp.inf)
        row_max = lax.optimization_barrier(jnp.max(masked, axis=2, keepdims=True))
        exponent = jnp.where(allowed[None], jnp.exp(masked - row_max), 0.0)
        row_total = lax.optimization_barrier(jnp.sum(exponent, axis=2, keepdims=True))
        weights = rounded(exponent)
        mixed_out = jnp.einsum('htw,whd->htd', weights, value_block) / row_total
        attn_block = mixed_out.transpose(1, 0, 2).astype(jnp.bfloat16)
        probability = exponent / row_total
        attn_wide = lax.optimization_barrier(attn_block).astype(jnp.float32)
        delta_rows = lax.optimization_barrier(jnp.sum(upstream * attn_wide, axis=2)).T[:, :, None]
        grad_probs = jnp.einsum('thd,whd->htw', upstream, value_block)
        grad_scores = rounded(probability * (grad_probs - delta_rows))
        grad_query = scale_factor * jnp.concatenate([jnp.einsum('htw,whd->thd', grad_scores, key_nope), jnp.einsum('htw,wd->thd', grad_scores, key_rope)], 2)
        term_nope = rounded(scale_factor * jnp.einsum('htw,thd->whd', grad_scores, query_nope))
        term_rope = rounded(scale_factor * jnp.einsum('htw,thd->whd', grad_scores, query_rope))
        term_value = rounded(jnp.einsum('htw,thd->whd', rounded(probability), upstream))
        grad_keys = lax.dynamic_update_slice_in_dim(grad_keys, lax.dynamic_slice_in_dim(grad_keys, row_start, window, 0) + term_nope.reshape(window, head_count * NOPE), row_start, 0)
        grad_values = lax.dynamic_update_slice_in_dim(grad_values, lax.dynamic_slice_in_dim(grad_values, row_start, window, 0) + term_value.reshape(window, head_count * VDIM), row_start, 0)
        grad_rope = lax.dynamic_update_slice_in_dim(grad_rope, lax.dynamic_slice_in_dim(grad_rope, row_start, window, 0) + lax.optimization_barrier(jnp.sum(term_rope, axis=1)), row_start, 0)
        return ((grad_keys, grad_values, grad_rope), (attn_block.reshape(TOK_DEV, head_count * VDIM), grad_query.astype(jnp.bfloat16).reshape(TOK_DEV, head_count * (NOPE + ROPE))))
    initial = (jnp.zeros((TOKENS + margin, head_count * NOPE), jnp.float32), jnp.zeros((TOKENS + margin, head_count * VDIM), jnp.float32), jnp.zeros((TOKENS + margin, ROPE), jnp.float32))
    sums, outputs = lax.scan(one_block, initial, jnp.arange(N_CTX, dtype=jnp.int32))
    attn_out = outputs[0].reshape(TOKENS, head_count * VDIM)
    grad_queries = outputs[1].reshape(TOKENS, head_count * (NOPE + ROPE))
    key_grad = sums[0][margin:]
    value_grad = sums[1][margin:]
    rope_grad = sums[2][margin:]
    highest = lax.Precision.HIGHEST
    nope_grad = jnp.dot(key_grad, w_key.astype(jnp.float32).T, precision=highest) + jnp.dot(value_grad, w_value.astype(jnp.float32).T, precision=highest)
    grad_latent = jnp.concatenate([nope_grad, rope_grad], 1).astype(jnp.bfloat16)
    latent_wide = latent_nope.astype(jnp.float32).T
    grad_w_key = jnp.dot(latent_wide, key_grad, precision=highest).astype(jnp.bfloat16)
    grad_w_value = jnp.dot(latent_wide, value_grad, precision=highest).astype(jnp.bfloat16)
    return (attn_out, grad_queries, grad_latent, grad_w_key, grad_w_value)
```

```python
import functools
import math

import jax
import jax.numpy as jnp
from jax import lax
from jax.experimental import pallas as pl
from jax.experimental.pallas import tpu as pltpu
from jax.sharding import PartitionSpec as P

LAT = 512
ROPE = 64
NOPE = 128
VDIM = 128
PREV = 4
NZ = 8
NY = 4
MESH = pl.DeviceIdType.MESH


def f32(x):
    return x.astype(jnp.float32)


def halo_kernel(n_ctx, latent_ref, window_ref, send_sem, recv_sem):
    me = lax.axis_index("ctx")

    barrier = pltpu.get_barrier_semaphore()
    for s in range(1, PREV + 1):

        @pl.when(me >= s)
        def _():
            pl.semaphore_signal(barrier, inc=1, device_id={"ctx": me - s}, device_id_type=MESH)

    @pl.when(me < n_ctx - 1)
    def _():
        pl.semaphore_wait(barrier, jnp.minimum(n_ctx - 1 - me, PREV))

    def copy(s):
        return pltpu.make_async_remote_copy(
            src_ref=latent_ref,
            dst_ref=window_ref.at[PREV - s],
            send_sem=send_sem.at[s - 1],
            recv_sem=recv_sem.at[s - 1],
            device_id={"ctx": me + s},
            device_id_type=MESH,
        )

    for s in range(1, PREV + 1):

        @pl.when(me + s < n_ctx)
        def _():
            copy(s).start()

    window_ref[PREV] = latent_ref[...]
    for s in range(1, PREV + 1):

        @pl.when(me >= s)
        def _():
            copy(s).wait_recv()

        @pl.when(me < s)
        def _():
            window_ref[PREV - s] = jnp.zeros_like(latent_ref)

    for s in range(1, PREV + 1):

        @pl.when(me + s < n_ctx)
        def _():
            copy(s).wait_send()


def reduce_kernel(
    n_ctx,
    n_head,
    gw_ref,
    gl_ref,
    gw_out,
    gl_out,
    pair_in,
    half,
    z_in,
    y_in,
    zy_in,
    yz_in,
    y_part,
    z_part,
    head_in,
    ctx_part,
    ctx_in,
    pair_s,
    pair_r,
    pairg_s,
    pairg_r,
    z_s,
    z_r,
    y_s,
    y_r,
    zy_s,
    zy_r,
    yz_s,
    yz_r,
    zyg_s,
    zyg_r,
    yzg_s,
    yzg_r,
    zg_s,
    zg_r,
    yg_s,
    yg_r,
    head_s,
    head_r,
    ctx_s,
    ctx_r,
    headg_s,
    headg_r,
):
    me = lax.axis_index("ctx")
    head = lax.axis_index("head")
    core = lax.rem(me, 2)
    z = lax.rem(me // 2, NZ)
    y = me // (2 * NZ)
    partner = me + 1 - 2 * core
    rows = gl_ref.shape[1] // n_head

    def at_z(s):
        return lax.rem(z + s, NZ)

    def at_y(s):
        return lax.rem(y + s, NY)

    def z_dev(s):
        return (y * NZ + at_z(s)) * 2 + core

    def y_dev(s):
        return (at_y(s) * NZ + z) * 2 + core

    def at_head(s):
        return lax.rem(head + s, n_head)

    barrier = pltpu.get_barrier_semaphore()

    def greet(device):
        pl.semaphore_signal(barrier, inc=1, device_id=device, device_id_type=MESH)

    greet({"ctx": partner})
    for s in range(1, NZ):
        greet({"ctx": z_dev(s)})
    for s in range(1, NY):
        greet({"ctx": y_dev(s)})
    for s in range(1, n_head):
        greet({"head": at_head(s)})
    for s in range(1, PREV + 1):

        @pl.when(me + s < n_ctx)
        def _():
            greet({"ctx": me + s})

    pl.semaphore_wait(barrier, 1 + NZ - 1 + NY - 1 + n_head - 1 + jnp.minimum(me, PREV))

    def remote(src, dst, send, recv, device):
        return pltpu.make_async_remote_copy(
            src_ref=src, dst_ref=dst, send_sem=send, recv_sem=recv, device_id=device, device_id_type=MESH
        )

    def mult(x, m):
        return pl.multiple_of(x, m)

    pair = remote(gw_ref.at[1 - core], pair_in, pair_s, pair_r, {"ctx": partner})
    pair.start()

    def head_copy(s):
        return remote(
            gl_ref.at[:, pl.ds(mult(at_head(s) * rows, rows), rows), :],
            head_in.at[s - 1],
            head_s.at[s - 1],
            head_r.at[s - 1],
            {"head": at_head(s)},
        )

    for s in range(1, n_head):
        head_copy(s).start()

    pair.wait_recv()
    half[...] = (f32(gw_ref[core]) + f32(pair_in[...])).astype(jnp.bfloat16)

    def z_copy(s):
        return remote(
            half.at[pl.ds(mult(at_z(s) * 32, 32), 32), :],
            z_in.at[s - 1],
            z_s.at[s - 1],
            z_r.at[s - 1],
            {"ctx": z_dev(s)},
        )

    def y_copy(s):
        return remote(
            half.at[pl.ds(mult(256 + at_y(s) * 64, 64), 64), :],
            y_in.at[s - 1],
            y_s.at[s - 1],
            y_r.at[s - 1],
            {"ctx": y_dev(s)},
        )

    for s in range(1, NZ):
        z_copy(s).start()
    for s in range(1, NY):
        y_copy(s).start()

    total = f32(gl_ref[:, pl.ds(mult(head * rows, rows), rows), :])
    for s in range(1, n_head):
        head_copy(s).wait_recv()
        total += f32(head_in[s - 1])
    ctx_part[...] = total.astype(jnp.bfloat16)

    def ctx_copy(s):
        return remote(
            ctx_part.at[PREV - s],
            ctx_in.at[s - 1],
            ctx_s.at[s - 1],
            ctx_r.at[s - 1],
            {"ctx": me - s},
        )

    for s in range(1, PREV + 1):

        @pl.when(me >= s)
        def _():
            ctx_copy(s).start()

    total = f32(half[pl.ds(mult(z * 32, 32), 32), :])
    for s in range(1, NZ):
        z_copy(s).wait_recv()
        total += f32(z_in[s - 1])
    z_part[...] = total.astype(jnp.bfloat16)

    def zy_copy(s):
        return remote(
            z_part.at[:, pl.ds(mult(at_y(s) * 128, 128), 128)],
            zy_in.at[s - 1],
            zy_s.at[s - 1],
            zy_r.at[s - 1],
            {"ctx": y_dev(s)},
        )

    for s in range(1, NY):
        zy_copy(s).start()

    total = f32(half[pl.ds(mult(256 + y * 64, 64), 64), :])
    for s in range(1, NY):
        y_copy(s).wait_recv()
        total += f32(y_in[s - 1])
    y_part[...] = total.astype(jnp.bfloat16)

    def small(zi):
        return pl.ds(mult(zi // 2 * 16, 16), 16), pl.ds(mult(lax.rem(zi, 2) * 256, 256), 256)

    def yz_copy(s):
        r, c = small(at_z(s))
        return remote(
            y_part.at[r, c],
            yz_in.at[s - 1],
            yz_s.at[s - 1],
            yz_r.at[s - 1],
            {"ctx": z_dev(s)},
        )

    for s in range(1, NZ):
        yz_copy(s).start()

    for s in range(1, PREV + 1):

        @pl.when(me + s < n_ctx)
        def _():
            ctx_copy(s).wait_recv()

        @pl.when(me + s >= n_ctx)
        def _():
            ctx_in[s - 1] = jnp.zeros(ctx_in.shape[1:], jnp.bfloat16)

    total = f32(ctx_part[PREV])
    for s in range(1, PREV + 1):
        total += f32(ctx_in[s - 1])
    my_rows = pl.ds(mult(head * rows, rows), rows)
    gl_out[my_rows, :] = total.astype(jnp.bfloat16)

    def headg_copy(s):
        return remote(
            gl_out.at[my_rows, :],
            gl_out.at[my_rows, :],
            headg_s.at[s - 1],
            headg_r.at[s - 1],
            {"head": at_head(s)},
        )

    for s in range(1, n_head):
        headg_copy(s).start()

    zrows = pl.ds(mult(z * 32, 32), 32)
    ycols = pl.ds(mult(y * 128, 128), 128)
    total = f32(z_part[:, ycols])
    for s in range(1, NY):
        zy_copy(s).wait_recv()
        total += f32(zy_in[s - 1])
    gw_out[core, zrows, ycols] = total.astype(jnp.bfloat16)

    def zyg_copy(s):
        block = gw_out.at[core, zrows, ycols]
        return remote(block, block, zyg_s.at[s - 1], zyg_r.at[s - 1], {"ctx": y_dev(s)})

    for s in range(1, NY):
        zyg_copy(s).start()

    r, c = small(z)
    total = f32(y_part[r, c])
    for s in range(1, NZ):
        yz_copy(s).wait_recv()
        total += f32(yz_in[s - 1])
    brows = pl.ds(mult(256 + y * 64 + z // 2 * 16, 16), 16)
    gw_out[core, brows, c] = total.astype(jnp.bfloat16)

    def yzg_copy(s):
        block = gw_out.at[core, brows, c]
        return remote(block, block, yzg_s.at[s - 1], yzg_r.at[s - 1], {"ctx": z_dev(s)})

    for s in range(1, NZ):
        yzg_copy(s).start()

    for s in range(1, NY):
        zyg_copy(s).wait_recv()

    def zg_copy(s):
        block = gw_out.at[core, zrows, :]
        return remote(block, block, zg_s.at[s - 1], zg_r.at[s - 1], {"ctx": z_dev(s)})

    for s in range(1, NZ):
        zg_copy(s).start()

    for s in range(1, NZ):
        yzg_copy(s).wait_recv()

    def yg_copy(s):
        block = gw_out.at[core, pl.ds(mult(256 + y * 64, 64), 64), :]
        return remote(block, block, yg_s.at[s - 1], yg_r.at[s - 1], {"ctx": y_dev(s)})

    for s in range(1, NY):
        yg_copy(s).start()

    for s in range(1, NZ):
        zg_copy(s).wait_recv()
    for s in range(1, NY):
        yg_copy(s).wait_recv()
    block = gw_out.at[core]
    pairg = remote(block, block, pairg_s, pairg_r, {"ctx": partner})
    pairg.start()
    pair.wait_send()

    for s in range(1, n_head):
        head_copy(s).wait_send()
        headg_copy(s).wait()
    for s in range(1, NZ):
        z_copy(s).wait_send()
        yz_copy(s).wait_send()
        yzg_copy(s).wait_send()
        zg_copy(s).wait_send()
    for s in range(1, NY):
        y_copy(s).wait_send()
        zy_copy(s).wait_send()
        zyg_copy(s).wait_send()
        yg_copy(s).wait_send()
    for s in range(1, PREV + 1):

        @pl.when(me >= s)
        def _():
            ctx_copy(s).wait_send()

    pairg.wait()


VMEM_SPEC = pl.BlockSpec(memory_space=pltpu.VMEM)


def halo(latent, n_ctx):
    tok, wide = latent.shape
    return pl.pallas_call(
        functools.partial(halo_kernel, n_ctx),
        out_shape=jax.ShapeDtypeStruct((PREV + 1, tok, wide), latent.dtype),
        in_specs=[VMEM_SPEC],
        out_specs=VMEM_SPEC,
        scratch_shapes=[pltpu.SemaphoreType.DMA((PREV,)), pltpu.SemaphoreType.DMA((PREV,))],
        compiler_params=pltpu.CompilerParams(collective_id=0, has_side_effects=True),
        name="halo",
    )(latent)


def reduce_all(gw, gl, n_ctx, n_head):
    tok, wide = gl.shape[1:]
    rows = tok // n_head
    bf = jnp.bfloat16

    def sems(n):
        return [pltpu.SemaphoreType.DMA((n,)), pltpu.SemaphoreType.DMA((n,))]

    return pl.pallas_call(
        functools.partial(reduce_kernel, n_ctx, n_head),
        out_shape=[
            jax.ShapeDtypeStruct(gw.shape, bf),
            jax.ShapeDtypeStruct((tok, wide), bf),
        ],
        in_specs=[VMEM_SPEC] * 2,
        out_specs=[VMEM_SPEC] * 2,
        scratch_shapes=[
            pltpu.VMEM((512, 512), bf),
            pltpu.VMEM((512, 512), bf),
            pltpu.VMEM((NZ - 1, 32, 512), bf),
            pltpu.VMEM((NY - 1, 64, 512), bf),
            pltpu.VMEM((NY - 1, 32, 128), bf),
            pltpu.VMEM((NZ - 1, 16, 256), bf),
            pltpu.VMEM((64, 512), bf),
            pltpu.VMEM((32, 512), bf),
            pltpu.VMEM((n_head - 1, PREV + 1, rows, wide), bf),
            pltpu.VMEM((PREV + 1, rows, wide), bf),
            pltpu.VMEM((PREV, rows, wide), bf),
            *[pltpu.SemaphoreType.DMA] * 4,
            *sems(NZ - 1),
            *sems(NY - 1),
            *sems(NY - 1),
            *sems(NZ - 1),
            *sems(NY - 1),
            *sems(NZ - 1),
            *sems(NZ - 1),
            *sems(NY - 1),
            *sems(n_head - 1),
            *sems(PREV),
            *sems(n_head - 1),
        ],
        compiler_params=pltpu.CompilerParams(
            collective_id=1, has_side_effects=True, vmem_limit_bytes=32 * 2**20
        ),
        name="reduce_all",
    )(gw, gl)


def per_device(queries, latent, w_key, w_value, grad_out, segment_ids):
    tok_rows = queries.shape[0]
    head_count = w_key.shape[1] // NOPE
    n_ctx = lax.axis_size("ctx")
    n_head = lax.axis_size("head")
    window = (PREV + 1) * tok_rows
    margin = PREV * tok_rows
    scale_factor = 1.0 / math.sqrt(NOPE + ROPE)
    position = lax.axis_index("ctx")
    window_all = halo(latent, n_ctx).reshape(window, LAT + ROPE)
    first_part = window_all[:, :LAT]
    window_rope = window_all[:, LAT:]
    key_flat = jnp.dot(first_part, w_key, preferred_element_type=jnp.float32).astype(jnp.bfloat16)
    value_flat = jnp.dot(first_part, w_value, preferred_element_type=jnp.float32).astype(
        jnp.bfloat16
    )
    key_nope = key_flat.reshape(window, head_count, NOPE)
    value_block = value_flat.reshape(window, head_count, VDIM)
    row_start = position * tok_rows
    query_pos = row_start + jnp.arange(tok_rows, dtype=jnp.int32)
    key_pos = row_start - margin + jnp.arange(window, dtype=jnp.int32)
    segment_padded = jnp.concatenate([jnp.full((margin,), -1, jnp.int32), segment_ids], 0)
    query_segment = lax.dynamic_slice_in_dim(segment_ids, row_start, tok_rows, 0)
    key_segment = lax.dynamic_slice_in_dim(segment_padded, row_start, window, 0)
    allowed = (
        (key_pos[None, :] <= query_pos[:, None])
        & (key_pos[None, :] >= 0)
        & (key_segment[None, :] == query_segment[:, None])
    )
    query_all = queries.reshape(tok_rows, head_count, NOPE + ROPE)
    query_nope = query_all[:, :, :NOPE]
    query_rope = query_all[:, :, NOPE:]
    upstream = grad_out.reshape(tok_rows, head_count, VDIM)
    scores = scale_factor * (
        jnp.einsum("thd,whd->htw", query_nope, key_nope, preferred_element_type=jnp.float32)
        + jnp.einsum("thd,wd->htw", query_rope, window_rope, preferred_element_type=jnp.float32)
    )
    masked = jnp.where(allowed[None], scores, -jnp.inf)
    row_max = jnp.max(masked, axis=2, keepdims=True)
    exponent = jnp.where(allowed[None], jnp.exp(masked - row_max), 0.0)
    row_total = jnp.sum(exponent, axis=2, keepdims=True)
    weights = exponent.astype(jnp.bfloat16)
    mixed_out = (
        jnp.einsum("htw,whd->htd", weights, value_block, preferred_element_type=jnp.float32)
        / row_total
    )
    attn_block = mixed_out.transpose(1, 0, 2).astype(jnp.bfloat16)
    probability = exponent / row_total
    delta_rows = jnp.sum(upstream.astype(jnp.float32) * attn_block.astype(jnp.float32), axis=2).T[
        :, :, None
    ]
    grad_probs = jnp.einsum(
        "thd,whd->htw", upstream, value_block, preferred_element_type=jnp.float32
    )
    grad_scores = (probability * (grad_probs - delta_rows)).astype(jnp.bfloat16)
    grad_query = scale_factor * jnp.concatenate(
        [
            jnp.einsum("htw,whd->thd", grad_scores, key_nope, preferred_element_type=jnp.float32),
            jnp.einsum("htw,wd->thd", grad_scores, window_rope, preferred_element_type=jnp.float32),
        ],
        2,
    )
    term_nope = (
        scale_factor
        * jnp.einsum("htw,thd->whd", grad_scores, query_nope, preferred_element_type=jnp.float32)
    ).astype(jnp.bfloat16)
    term_rope = (
        scale_factor
        * jnp.einsum("htw,thd->whd", grad_scores, query_rope, preferred_element_type=jnp.float32)
    ).astype(jnp.bfloat16)
    term_value = jnp.einsum(
        "htw,thd->whd",
        probability.astype(jnp.bfloat16),
        upstream,
        preferred_element_type=jnp.float32,
    ).astype(jnp.bfloat16)
    rope_term = jnp.sum(term_rope.astype(jnp.float32), axis=1)
    nope_flat = term_nope.reshape(window, head_count * NOPE)
    value_flat_grad = term_value.reshape(window, head_count * VDIM)
    first_term = jnp.dot(nope_flat, w_key.T, preferred_element_type=jnp.float32) + jnp.dot(
        value_flat_grad, w_value.T, preferred_element_type=jnp.float32
    )
    weight_key = jnp.dot(first_part.T, nope_flat, preferred_element_type=jnp.float32)
    weight_value = jnp.dot(first_part.T, value_flat_grad, preferred_element_type=jnp.float32)
    gw = jnp.stack([weight_key.astype(jnp.bfloat16), weight_value.astype(jnp.bfloat16)])
    gl = jnp.concatenate([first_term, rope_term], 1).astype(jnp.bfloat16)
    gw_sum, grad_latent = reduce_all(
        gw, gl.reshape(PREV + 1, tok_rows, LAT + ROPE), n_ctx, n_head
    )
    attn_out = attn_block.reshape(tok_rows, head_count * VDIM)
    grad_queries = grad_query.astype(jnp.bfloat16).reshape(tok_rows, head_count * (NOPE + ROPE))
    return (attn_out, grad_queries, grad_latent, gw_sum[0], gw_sum[1])


def solution(mesh):
    return jax.shard_map(
        per_device,
        mesh=mesh,
        in_specs=(
            P("ctx", "head"),
            P("ctx", None),
            P(None, "head"),
            P(None, "head"),
            P("ctx", "head"),
            P(),
        ),
        out_specs=(
            P("ctx", "head"),
            P("ctx", "head"),
            P("ctx", None),
            P(None, "head"),
            P(None, "head"),
        ),
        check_vma=False,
    )
```

```python
import functools
import math

import jax
import jax.numpy as jnp
from jax import lax
from jax.experimental import pallas as pl
from jax.experimental.pallas import tpu as pltpu
from jax.sharding import PartitionSpec as P

LAT = 512
ROPE = 64
NOPE = 128
VDIM = 128
PREV = 4
NZ = 8
NY = 4
TOK = 128
WIN = (PREV + 1) * TOK
QK = NOPE + ROPE
HEADS = 4
PIECES = 2
COLS = HEADS // PIECES * NOPE
MESH = pl.DeviceIdType.MESH
BF = jnp.bfloat16
SCALE = 1.0 / math.sqrt(QK)


def f32(x):
    return x.astype(jnp.float32)


def nn(a, b):
    return jnp.dot(a, b, preferred_element_type=jnp.float32)


def nt(a, b):
    return lax.dot_general(a, b, (((1,), (1,)), ((), ())), preferred_element_type=jnp.float32)


def mult(x, m):
    return pl.multiple_of(x, m)


def slot_cols(slot):
    return pl.ds(slot * TOK, TOK)


def kernel(n_ctx, n_head, *refs):
    (
        q_hbm,
        lat_ref,
        wk_hbm,
        wv_hbm,
        do_hbm,
        seg_ref,
        attn_ref,
        gq_ref,
        gl_out,
        gw_out,
        q_ref,
        wcat,
        do_ref,
        win,
        wt,
        qs,
        qt,
        dot,
        kt,
        vt,
        bias,
        dcat,
        rope_sum,
        part,
        pair_in,
        half,
        z_in,
        y_in,
        zy_in,
        yz_in,
        z_part,
        y_part,
        glb,
        head_in,
        ctx_part,
        ctx_in,
        load_sem,
        halo_s,
        halo_r,
        mate_s,
        mate_r,
        pair_s,
        pair_r,
        z_s,
        z_r,
        y_s,
        y_r,
        zy_s,
        zy_r,
        yz_s,
        yz_r,
        zyg_s,
        zyg_r,
        yzg_s,
        yzg_r,
        zg_s,
        zg_r,
        yg_s,
        yg_r,
        pairg_s,
        pairg_r,
        head_s,
        head_r,
        ctx_s,
        ctx_r,
        headg_s,
        headg_r,
    ) = refs
    me = lax.axis_index("ctx")
    head = lax.axis_index("head")
    core = lax.rem(me, 2)
    z = lax.rem(me // 2, NZ)
    y = me // (2 * NZ)
    partner = me + 1 - 2 * core
    rows = glb.shape[0] // n_head

    def z_dev(s):
        return {"ctx": (y * NZ + lax.rem(z + s, NZ)) * 2 + core}

    def y_dev(s):
        return {"ctx": (lax.rem(y + s, NY) * NZ + z) * 2 + core}

    def at_head(s):
        return lax.rem(head + s, n_head)

    def remote(src, dst, send, recv, device):
        return pltpu.make_async_remote_copy(
            src_ref=src, dst_ref=dst, send_sem=send, recv_sem=recv, device_id=device, device_id_type=MESH
        )

    loads = [
        pltpu.make_async_copy(src, dst, load_sem.at[i])
        for i, (src, dst) in enumerate(
            [(q_hbm, q_ref), (do_hbm, do_ref)]
            + [
                (w.at[:, pl.ds(p * COLS, COLS)], wcat.at[:, pl.ds((2 * p + kind) * COLS, COLS)])
                for p in range(PIECES)
                for kind, w in enumerate((wk_hbm, wv_hbm))
            ]
        )
    ]
    for load in loads:
        load.start()

    barrier = pltpu.get_barrier_semaphore()

    def greet(device):
        pl.semaphore_signal(barrier, inc=1, device_id=device, device_id_type=MESH)

    for s in range(1, PREV + 1):

        @pl.when(me >= s)
        def _():
            greet({"ctx": me - s})

        @pl.when(me + s < n_ctx)
        def _():
            greet({"ctx": me + s})

    greet({"ctx": partner})
    for s in range(1, NZ):
        greet(z_dev(s))
    for s in range(1, NY):
        greet(y_dev(s))
    for s in range(1, n_head):
        greet({"head": at_head(s)})
    pl.semaphore_wait(
        barrier,
        NZ - 1 + NY - 1 + n_head + jnp.minimum(me, PREV) + jnp.minimum(n_ctx - 1 - me, PREV),
    )

    def halo_copy(i):
        d = 2 * (i + 1)
        return remote(
            lat_ref, win.at[:, slot_cols(PREV - d)], halo_s.at[i], halo_r.at[i], {"ctx": me + d}
        )

    def mate_copy(i, src):
        return remote(
            src, win.at[:, slot_cols(PREV - 1 - 2 * i)], mate_s.at[i], mate_r.at[i], {"ctx": partner}
        )

    for i in range(2):

        @pl.when(me + 2 * (i + 1) < n_ctx)
        def _():
            halo_copy(i).start()

    @pl.when(core == 0)
    def _():
        mate_copy(0, lat_ref).start()

    win[:, slot_cols(PREV)] = lat_ref[...]
    for load in loads:
        load.wait()
    for i in range(2 * PIECES):
        wt[pl.ds(i * COLS, COLS), :] = wcat[:, pl.ds(i * COLS, COLS)].T
    for h in range(HEADS):
        block = q_ref[:, pl.ds(h * QK, QK)]
        qs[h] = block
        qt[h] = block.T
        dot[h] = do_ref[:, pl.ds(h * VDIM, VDIM)].T
    own = seg_ref[pl.ds(me, 1), :]
    query_seg = jnp.broadcast_to(own, (TOK, TOK)).T
    for s in range(PREV + 1):
        place = me - PREV + s
        key_seg = jnp.where(place >= 0, seg_ref[pl.ds(jnp.maximum(place, 0), 1), :], -1)
        allowed = query_seg == key_seg
        if s == PREV:
            allowed &= lax.broadcasted_iota(jnp.int32, (TOK, TOK), 1) <= lax.broadcasted_iota(
                jnp.int32, (TOK, TOK), 0
            )
        bias[:, slot_cols(s)] = jnp.where(allowed, 0.0, -jnp.inf)

    def project(start, size):
        cols = pl.ds(start, size)
        for h in range(HEADS):
            p, j = divmod(h, HEADS // PIECES)
            base = 2 * p * COLS + j * NOPE
            kt[h, pl.ds(0, NOPE), cols] = nn(wt[pl.ds(base, NOPE), :], win[pl.ds(0, LAT), cols]).astype(BF)
            kt[h, pl.ds(NOPE, ROPE), cols] = win[pl.ds(LAT, ROPE), cols]
            vt[h, :, cols] = nn(wt[pl.ds(base + COLS, NOPE), :], win[pl.ds(0, LAT), cols]).astype(BF)

    project(PREV * TOK, TOK)

    def arrived(i):
        d = 2 * (i + 1)

        @pl.when(me >= d)
        def _():
            halo_copy(i).wait_recv()

        @pl.when(me < d)
        def _():
            win[:, slot_cols(PREV - d)] = jnp.zeros((LAT + ROPE, TOK), BF)

    arrived(0)

    @pl.when(core == 0)
    def _():
        mate_copy(1, win.at[:, slot_cols(2)]).start()

    @pl.when(core == 1)
    def _():
        mate_copy(0, win.at[:, slot_cols(2)]).start()

    arrived(1)

    @pl.when(core == 1)
    def _():
        mate_copy(1, win.at[:, slot_cols(0)]).start()

    for i in range(2):
        mate_copy(i, lat_ref).wait_recv()
    project(0, PREV * TOK)

    def one_head(h):
        p, j = divmod(h, HEADS // PIECES)
        base = 2 * p * COLS + j * NOPE
        scores = nn(qs[h], kt[h]) * SCALE + bias[...]
        expo = jnp.exp(scores - jnp.max(scores, axis=1, keepdims=True))
        scaling = 1.0 / jnp.sum(expo, axis=1, keepdims=True)
        out = (nt(expo.astype(BF), vt[h]) * scaling).astype(BF)
        attn_ref[:, pl.ds(h * VDIM, VDIM)] = out
        upstream = do_ref[:, pl.ds(h * VDIM, VDIM)]
        delta = jnp.sum(f32(upstream) * f32(out), axis=1, keepdims=True)
        probs = expo * scaling
        grad_scores = (probs * (nn(upstream, vt[h]) - delta)).astype(BF)
        gq_ref[:, pl.ds(h * QK, QK)] = (nt(grad_scores, kt[h]) * SCALE).astype(BF)
        term = (nn(qt[h], grad_scores) * SCALE).astype(BF)
        dcat[pl.ds(base, NOPE), :] = term[:NOPE]
        rope_sum[...] = f32(term[NOPE:]) if h == 0 else rope_sum[...] + f32(term[NOPE:])
        dcat[pl.ds(base + COLS, VDIM), :] = nn(dot[h], probs.astype(BF)).astype(BF)

    def pair_copy(p):
        return remote(
            part.at[p, 1 - core], pair_in.at[p], pair_s.at[p], pair_r.at[p], {"ctx": partner}
        )

    def weight_terms(p):
        terms = nt(win[pl.ds(0, LAT), :], dcat[pl.ds(2 * p * COLS, 2 * COLS), :]).astype(BF)
        part[p, 0] = terms[:, :COLS]
        part[p, 1] = terms[:, COLS:]
        pair_copy(p).start()

    def z_copy(p, s):
        block = pl.ds(mult(lax.rem(z + s, NZ) * 32, 32), 32)
        return remote(half.at[p, block], z_in.at[p, s - 1], z_s.at[p, s - 1], z_r.at[p, s - 1], z_dev(s))

    def y_copy(p, s):
        block = pl.ds(mult(256 + lax.rem(y + s, NY) * 64, 64), 64)
        return remote(half.at[p, block], y_in.at[p, s - 1], y_s.at[p, s - 1], y_r.at[p, s - 1], y_dev(s))

    def small(i):
        return pl.ds(mult(i // 2 * 16, 16), 16), pl.ds(mult(lax.rem(i, 2) * 128, 128), 128)

    def zy_copy(p, s):
        r, c = small(lax.rem(y + s, NY))
        return remote(z_part.at[p, r, c], zy_in.at[p, s - 1], zy_s.at[p, s - 1], zy_r.at[p, s - 1], y_dev(s))

    def yz_copy(p, s):
        r, c = small(lax.rem(z + s, NZ))
        return remote(y_part.at[p, r, c], yz_in.at[p, s - 1], yz_s.at[p, s - 1], yz_r.at[p, s - 1], z_dev(s))

    def z_place(p):
        return gw_out.at[core, pl.ds(mult(z * 32, 32), 32), pl.ds(p * COLS, COLS)]

    def y_place(p):
        return gw_out.at[core, pl.ds(mult(256 + y * 64, 64), 64), pl.ds(p * COLS, COLS)]

    def zy_place(p):
        r = pl.ds(mult(z * 32 + y // 2 * 16, 16), 16)
        return gw_out.at[core, r, pl.ds(mult(p * COLS + lax.rem(y, 2) * 128, 128), 128)]

    def yz_place(p):
        r = pl.ds(mult(256 + y * 64 + z // 2 * 16, 16), 16)
        return gw_out.at[core, r, pl.ds(mult(p * COLS + lax.rem(z, 2) * 128, 128), 128)]

    def zyg_copy(p, s):
        return remote(zy_place(p), zy_place(p), zyg_s.at[p, s - 1], zyg_r.at[p, s - 1], y_dev(s))

    def yzg_copy(p, s):
        return remote(yz_place(p), yz_place(p), yzg_s.at[p, s - 1], yzg_r.at[p, s - 1], z_dev(s))

    def zg_copy(p, s):
        return remote(z_place(p), z_place(p), zg_s.at[p, s - 1], zg_r.at[p, s - 1], z_dev(s))

    def yg_copy(p, s):
        return remote(y_place(p), y_place(p), yg_s.at[p, s - 1], yg_r.at[p, s - 1], y_dev(s))

    def pairg_copy(p):
        block = gw_out.at[core, :, pl.ds(p * COLS, COLS)]
        return remote(block, block, pairg_s.at[p], pairg_r.at[p], {"ctx": partner})

    def stage_a(p):
        pair_copy(p).wait_recv()
        half[p] = (f32(part[p, core]) + f32(pair_in[p])).astype(BF)
        for s in range(1, NZ):
            z_copy(p, s).start()
        for s in range(1, NY):
            y_copy(p, s).start()

    def stage_b(p):
        total = f32(half[p, pl.ds(mult(z * 32, 32), 32), :])
        for s in range(1, NZ):
            z_copy(p, s).wait_recv()
            total += f32(z_in[p, s - 1])
        z_part[p] = total.astype(BF)
        for s in range(1, NY):
            zy_copy(p, s).start()
        total = f32(half[p, pl.ds(mult(256 + y * 64, 64), 64), :])
        for s in range(1, NY):
            y_copy(p, s).wait_recv()
            total += f32(y_in[p, s - 1])
        y_part[p] = total.astype(BF)
        for s in range(1, NZ):
            yz_copy(p, s).start()

    def stage_c(p):
        r, c = small(y)
        total = f32(z_part[p, r, c])
        for s in range(1, NY):
            zy_copy(p, s).wait_recv()
            total += f32(zy_in[p, s - 1])
        zy_place(p)[...] = total.astype(BF)
        for s in range(1, NY):
            zyg_copy(p, s).start()
        r, c = small(z)
        total = f32(y_part[p, r, c])
        for s in range(1, NZ):
            yz_copy(p, s).wait_recv()
            total += f32(yz_in[p, s - 1])
        yz_place(p)[...] = total.astype(BF)
        for s in range(1, NZ):
            yzg_copy(p, s).start()

    def stage_d(p):
        for s in range(1, NY):
            zyg_copy(p, s).wait_recv()
        for s in range(1, NZ):
            zg_copy(p, s).start()
        for s in range(1, NZ):
            yzg_copy(p, s).wait_recv()
        for s in range(1, NY):
            yg_copy(p, s).start()

    def stage_e(p):
        for s in range(1, NZ):
            zg_copy(p, s).wait_recv()
        for s in range(1, NY):
            yg_copy(p, s).wait_recv()
        pairg_copy(p).start()

    def head_copy(s):
        block = pl.ds(mult(at_head(s) * rows, 16), rows)
        return remote(
            glb.at[block], head_in.at[s - 1], head_s.at[s - 1], head_r.at[s - 1], {"head": at_head(s)}
        )

    def ctx_copy(s):
        return remote(
            ctx_part.at[:, slot_cols(PREV - s)],
            ctx_in.at[s - 1],
            ctx_s.at[s - 1],
            ctx_r.at[s - 1],
            {"ctx": me - s},
        )

    def headg_copy(s):
        block = gl_out.at[pl.ds(mult(head * rows, 16), rows)]
        return remote(block, block, headg_s.at[s - 1], headg_r.at[s - 1], {"head": at_head(s)})

    def latent_terms():
        glb[pl.ds(0, LAT), :] = nn(wcat[...], dcat[...]).astype(BF)
        glb[pl.ds(LAT, ROPE), :] = rope_sum[...].astype(BF)
        glb[pl.ds(LAT + ROPE, glb.shape[0] - LAT - ROPE), :] = jnp.zeros(
            (glb.shape[0] - LAT - ROPE, WIN), BF
        )
        for s in range(1, n_head):
            head_copy(s).start()

    def latent_heads():
        total = f32(glb[pl.ds(mult(head * rows, 16), rows), :])
        for s in range(1, n_head):
            head_copy(s).wait_recv()
            total += f32(head_in[s - 1])
        ctx_part[...] = total.astype(BF)
        for s in range(1, PREV + 1):

            @pl.when(me >= s)
            def _():
                ctx_copy(s).start()

    def latent_blocks():
        for s in range(1, PREV + 1):

            @pl.when(me + s < n_ctx)
            def _():
                ctx_copy(s).wait_recv()

            @pl.when(me + s >= n_ctx)
            def _():
                ctx_in[s - 1] = jnp.zeros(ctx_in.shape[1:], BF)

        total = f32(ctx_part[:, slot_cols(PREV)])
        for s in range(1, PREV + 1):
            total += f32(ctx_in[s - 1])
        gl_out[pl.ds(mult(head * rows, 16), rows), :] = total.astype(BF)
        for s in range(1, n_head):
            headg_copy(s).start()

    one_head(0)
    one_head(1)
    weight_terms(0)
    one_head(2)
    stage_a(0)
    one_head(3)
    weight_terms(1)
    latent_terms()
    stage_a(1)
    stage_b(0)
    latent_heads()
    stage_b(1)
    stage_c(0)
    latent_blocks()
    stage_c(1)
    stage_d(0)
    stage_d(1)
    stage_e(0)
    stage_e(1)

    for i in range(2):

        @pl.when(me + 2 * (i + 1) < n_ctx)
        def _():
            halo_copy(i).wait_send()

        mate_copy(i, lat_ref).wait_send()
    for s in range(1, n_head):
        head_copy(s).wait_send()
        headg_copy(s).wait()
    for s in range(1, PREV + 1):

        @pl.when(me >= s)
        def _():
            ctx_copy(s).wait_send()

    for p in range(PIECES):
        pair_copy(p).wait_send()
        for s in range(1, NZ):
            z_copy(p, s).wait_send()
            yz_copy(p, s).wait_send()
            yzg_copy(p, s).wait_send()
            zg_copy(p, s).wait_send()
        for s in range(1, NY):
            y_copy(p, s).wait_send()
            zy_copy(p, s).wait_send()
            zyg_copy(p, s).wait_send()
            yg_copy(p, s).wait_send()
        pairg_copy(p).wait()


def per_device(queries, latent, w_key, w_value, grad_out, segment_ids):
    n_ctx = lax.axis_size("ctx")
    n_head = lax.axis_size("head")
    vmem = pl.BlockSpec(memory_space=pltpu.VMEM)
    hbm = pl.BlockSpec(memory_space=pl.ANY)
    dma = pltpu.SemaphoreType.DMA
    rows = 80

    def buf(*shape, dtype=BF):
        return pltpu.VMEM(shape, dtype)

    def sems(*shape):
        return [dma(shape), dma(shape)]

    attn_out, grad_queries, grad_latent, grad_w = pl.pallas_call(
        functools.partial(kernel, n_ctx, n_head),
        out_shape=[
            jax.ShapeDtypeStruct((TOK, HEADS * VDIM), BF),
            jax.ShapeDtypeStruct((TOK, HEADS * QK), BF),
            jax.ShapeDtypeStruct((rows * n_head, TOK), BF),
            jax.ShapeDtypeStruct((2, LAT, HEADS * NOPE), BF),
        ],
        in_specs=[hbm, vmem, hbm, hbm, hbm, vmem],
        out_specs=[vmem] * 4,
        scratch_shapes=[
            buf(TOK, HEADS * QK),
            buf(LAT, 2 * HEADS * NOPE),
            buf(TOK, HEADS * VDIM),
            buf(LAT + ROPE, WIN),
            buf(2 * HEADS * NOPE, LAT),
            buf(HEADS, TOK, QK),
            buf(HEADS, QK, TOK),
            buf(HEADS, VDIM, TOK),
            buf(HEADS, QK, WIN),
            buf(HEADS, VDIM, WIN),
            buf(TOK, WIN, dtype=jnp.float32),
            buf(2 * HEADS * NOPE, WIN),
            buf(ROPE, WIN, dtype=jnp.float32),
            buf(PIECES, 2, LAT, COLS),
            buf(PIECES, LAT, COLS),
            buf(PIECES, LAT, COLS),
            buf(PIECES, NZ - 1, 32, COLS),
            buf(PIECES, NY - 1, 64, COLS),
            buf(PIECES, NY - 1, 16, 128),
            buf(PIECES, NZ - 1, 16, 128),
            buf(PIECES, 32, COLS),
            buf(PIECES, 64, COLS),
            buf(rows * n_head, WIN),
            buf(n_head - 1, rows, WIN),
            buf(rows, WIN),
            buf(PREV, rows, TOK),
            dma((2 + 2 * PIECES,)),
            *sems(2),
            *sems(2),
            *sems(PIECES),
            *sems(PIECES, NZ - 1),
            *sems(PIECES, NY - 1),
            *sems(PIECES, NY - 1),
            *sems(PIECES, NZ - 1),
            *sems(PIECES, NY - 1),
            *sems(PIECES, NZ - 1),
            *sems(PIECES, NZ - 1),
            *sems(PIECES, NY - 1),
            *sems(PIECES),
            *sems(n_head - 1),
            *sems(PREV),
            *sems(n_head - 1),
        ],
        compiler_params=pltpu.CompilerParams(
            collective_id=0, has_side_effects=True, vmem_limit_bytes=48 * 2**20
        ),
        name="attention",
    )(queries, latent.T, w_key, w_value, grad_out, segment_ids.reshape(n_ctx, TOK))
    return (attn_out, grad_queries, grad_latent[: LAT + ROPE].T, grad_w[0], grad_w[1])


def solution(mesh):
    return jax.shard_map(
        per_device,
        mesh=mesh,
        in_specs=(
            P("ctx", "head"),
            P("ctx", None),
            P(None, "head"),
            P(None, "head"),
            P("ctx", "head"),
            P(),
        ),
        out_specs=(
            P("ctx", "head"),
            P("ctx", "head"),
            P("ctx", None),
            P(None, "head"),
            P(None, "head"),
        ),
        check_vma=False,
    )
```

```python
import functools
import math

import jax
import jax.numpy as jnp
from jax import lax
from jax.experimental import pallas as pl
from jax.experimental.pallas import tpu as pltpu
from jax.sharding import PartitionSpec as P

LAT = 512
ROPE = 64
NOPE = 128
VDIM = 128
PREV = 4
NZ = 8
NY = 4
TOK = 128
WIN = (PREV + 1) * TOK
QK = NOPE + ROPE
HEADS = 4
PIECES = 2
COLS = HEADS // PIECES * NOPE
MESH = pl.DeviceIdType.MESH
BF = jnp.bfloat16
SCALE = 1.0 / math.sqrt(QK)


def f32(x):
    return x.astype(jnp.float32)


def nn(a, b):
    return jnp.dot(a, b, preferred_element_type=jnp.float32)


def nt(a, b):
    return lax.dot_general(a, b, (((1,), (1,)), ((), ())), preferred_element_type=jnp.float32)


def mult(x, m):
    return pl.multiple_of(x, m)


def slot_cols(slot):
    return pl.ds(slot * TOK, TOK)


def kernel(n_ctx, n_head, *refs):
    (
        q_hbm,
        lat_hbm,
        wk_hbm,
        wv_hbm,
        do_hbm,
        seg_hbm,
        attn_ref,
        gq_ref,
        gl_out,
        gw_out,
        q_ref,
        wcat,
        do_ref,
        seg_ref,
        win,
        wt,
        qs,
        qt,
        dot,
        kt,
        vt,
        bias,
        dcat,
        rope_sum,
        part,
        pair_in,
        half,
        z_in,
        y_in,
        zy_in,
        yz_in,
        z_part,
        y_part,
        glb,
        x_in,
        x_part,
        yl_in,
        ctx_part,
        ctx_in,
        load_sem,
        halo_s,
        halo_r,
        far_s,
        far_r,
        mate_s,
        mate_r,
        pair_s,
        pair_r,
        z_s,
        z_r,
        y_s,
        y_r,
        zy_s,
        zy_r,
        yz_s,
        yz_r,
        zyg_s,
        zyg_r,
        yzg_s,
        yzg_r,
        zg_s,
        zg_r,
        yg_s,
        yg_r,
        pairg_s,
        pairg_r,
        x_s,
        x_r,
        yl_s,
        yl_r,
        ctx_s,
        ctx_r,
        headg_s,
        headg_r,
    ) = refs
    me = lax.axis_index("ctx")
    head = lax.axis_index("head")
    core = lax.rem(me, 2)
    z = lax.rem(me // 2, NZ)
    y = me // (2 * NZ)
    partner = me + 1 - 2 * core
    rows = glb.shape[0] // n_head
    x = head // 2
    y_lo = lax.rem(head, 2)
    head_rows = pl.ds(mult(head * rows, 16), rows)

    def z_dev(s):
        return {"ctx": (y * NZ + lax.rem(z + s, NZ)) * 2 + core}

    def y_dev(s):
        return {"ctx": (lax.rem(y + s, NY) * NZ + z) * 2 + core}

    def at_head(s):
        return lax.rem(head + s, n_head)

    def remote(src, dst, send, recv, device):
        return pltpu.make_async_remote_copy(
            src_ref=src, dst_ref=dst, send_sem=send, recv_sem=recv, device_id=device, device_id_type=MESH
        )

    pad = pl.ds(LAT + ROPE, win.shape[0] - LAT - ROPE)
    win[pad, slot_cols(PREV)] = jnp.zeros((win.shape[0] - LAT - ROPE, TOK), BF)
    live = pl.ds(0, LAT + ROPE)
    own_block = win.at[live, slot_cols(PREV)]
    loads = [
        pltpu.make_async_copy(src, dst, load_sem.at[i])
        for i, (src, dst) in enumerate(
            [(lat_hbm, own_block), (seg_hbm, seg_ref), (q_hbm, q_ref), (do_hbm, do_ref)]
            + [
                (w.at[:, pl.ds(p * COLS, COLS)], wcat.at[:, pl.ds((2 * p + kind) * COLS, COLS)])
                for p in range(PIECES)
                for kind, w in enumerate((wk_hbm, wv_hbm))
            ]
        )
    ]
    for load in loads:
        load.start()

    barrier = pltpu.get_barrier_semaphore()

    def greet(device):
        pl.semaphore_signal(barrier, inc=1, device_id=device, device_id_type=MESH)

    for s in range(1, PREV + 1):

        @pl.when(me >= s)
        def _():
            greet({"ctx": me - s})

        @pl.when(me + s < n_ctx)
        def _():
            greet({"ctx": me + s})

    greet({"ctx": partner})
    for s in range(1, NZ):
        greet(z_dev(s))
    for s in range(1, NY):
        greet(y_dev(s))
    for s in range(1, n_head):
        greet({"head": at_head(s)})
    pl.semaphore_wait(
        barrier,
        NZ - 1 + NY - 1 + n_head + jnp.minimum(me, PREV) + jnp.minimum(n_ctx - 1 - me, PREV),
    )

    near = remote(
        own_block, win.at[live, slot_cols(2)], halo_s.at[0], halo_r.at[0], {"ctx": me + 2}
    )
    far = remote(
        win.at[head_rows, slot_cols(PREV)],
        win.at[head_rows, slot_cols(0)],
        halo_s.at[1],
        halo_r.at[1],
        {"ctx": me + 4},
    )

    def far_copy(s):
        block = win.at[head_rows, slot_cols(0)]
        return remote(block, block, far_s.at[s - 1], far_r.at[s - 1], {"head": at_head(s)})

    def mate_copy(i, src):
        return remote(
            win.at[live, slot_cols(src)],
            win.at[live, slot_cols(PREV - 1 - 2 * i)],
            mate_s.at[i],
            mate_r.at[i],
            {"ctx": partner},
        )

    loads[0].wait()

    @pl.when(me + 4 < n_ctx)
    def _():
        far.start()

    @pl.when(me + 2 < n_ctx)
    def _():
        near.start()

    @pl.when(core == 0)
    def _():
        mate_copy(0, PREV).start()

    for load in loads[1:]:
        load.wait()
    for i in range(2 * PIECES):
        wt[pl.ds(i * COLS, COLS), :] = wcat[:, pl.ds(i * COLS, COLS)].T
    for h in range(HEADS):
        block = q_ref[:, pl.ds(h * QK, QK)]
        qs[h] = block
        qt[h] = block.T
        dot[h] = do_ref[:, pl.ds(h * VDIM, VDIM)].T
    own = seg_ref[pl.ds(me, 1), :]
    query_seg = jnp.broadcast_to(own, (TOK, TOK)).T
    for s in range(PREV + 1):
        place = me - PREV + s
        key_seg = jnp.where(place >= 0, seg_ref[pl.ds(jnp.maximum(place, 0), 1), :], -1)
        allowed = query_seg == key_seg
        if s == PREV:
            allowed &= lax.broadcasted_iota(jnp.int32, (TOK, TOK), 1) <= lax.broadcasted_iota(
                jnp.int32, (TOK, TOK), 0
            )
        bias[:, slot_cols(s)] = jnp.where(allowed, 0.0, -jnp.inf)

    def project(start, size):
        cols = pl.ds(start, size)
        each = HEADS // PIECES
        for p in range(PIECES):
            made = nn(wt[pl.ds(2 * p * COLS, 2 * COLS), :], win[pl.ds(0, LAT), cols]).astype(BF)
            for j in range(each):
                kt[p * each + j, pl.ds(0, NOPE), cols] = made[j * NOPE : (j + 1) * NOPE]
                vt[p * each + j, :, cols] = made[COLS + j * VDIM : COLS + (j + 1) * VDIM]
        for h in range(HEADS):
            kt[h, pl.ds(NOPE, ROPE), cols] = win[pl.ds(LAT, ROPE), cols]

    project(PREV * TOK, TOK)

    @pl.when(me >= 4)
    def _():
        far.wait_recv()
        for s in range(1, n_head):
            far_copy(s).start()

    @pl.when(me >= 2)
    def _():
        near.wait_recv()

    @pl.when(me < 2)
    def _():
        win[live, slot_cols(2)] = jnp.zeros((LAT + ROPE, TOK), BF)

    @pl.when(core == 0)
    def _():
        mate_copy(1, 2).start()

    @pl.when(core == 1)
    def _():
        mate_copy(0, 2).start()

    mate_copy(0, PREV).wait_recv()
    project(2 * TOK, 2 * TOK)

    @pl.when(me >= 4)
    def _():
        for s in range(1, n_head):
            far_copy(s).wait_recv()

    @pl.when(me < 4)
    def _():
        win[live, slot_cols(0)] = jnp.zeros((LAT + ROPE, TOK), BF)

    @pl.when(core == 1)
    def _():
        mate_copy(1, 0).start()

    mate_copy(1, PREV).wait_recv()
    project(0, 2 * TOK)

    def one_head(h):
        p, j = divmod(h, HEADS // PIECES)
        base = 2 * p * COLS + j * NOPE
        scores = nn(qs[h], kt[h]) * SCALE + bias[...]
        expo = jnp.exp(scores - jnp.max(scores, axis=1, keepdims=True))
        scaling = 1.0 / jnp.sum(expo, axis=1, keepdims=True)
        out = (nt(expo.astype(BF), vt[h]) * scaling).astype(BF)
        attn_ref[:, pl.ds(h * VDIM, VDIM)] = out
        upstream = do_ref[:, pl.ds(h * VDIM, VDIM)]
        delta = jnp.sum(f32(upstream) * f32(out), axis=1, keepdims=True)
        probs = expo * scaling
        grad_scores = (probs * (nn(upstream, vt[h]) - delta)).astype(BF)
        gq_ref[:, pl.ds(h * QK, QK)] = (nt(grad_scores, kt[h]) * SCALE).astype(BF)
        term = (nn(qt[h], grad_scores) * SCALE).astype(BF)
        dcat[pl.ds(base, NOPE), :] = term[:NOPE]
        rope_sum[...] = f32(term[NOPE:]) if h == 0 else rope_sum[...] + f32(term[NOPE:])
        dcat[pl.ds(base + COLS, VDIM), :] = nn(dot[h], probs.astype(BF)).astype(BF)

    def pair_copy(p):
        return remote(
            part.at[p, 1 - core], pair_in.at[p], pair_s.at[p], pair_r.at[p], {"ctx": partner}
        )

    def weight_terms(p):
        terms = nt(win[pl.ds(0, LAT), :], dcat[pl.ds(2 * p * COLS, 2 * COLS), :]).astype(BF)
        part[p, 0] = terms[:, :COLS]
        part[p, 1] = terms[:, COLS:]
        pair_copy(p).start()

    def z_copy(p, s):
        block = pl.ds(mult(lax.rem(z + s, NZ) * 32, 32), 32)
        return remote(half.at[p, block], z_in.at[p, s - 1], z_s.at[p, s - 1], z_r.at[p, s - 1], z_dev(s))

    def y_copy(p, s):
        block = pl.ds(mult(256 + lax.rem(y + s, NY) * 64, 64), 64)
        return remote(half.at[p, block], y_in.at[p, s - 1], y_s.at[p, s - 1], y_r.at[p, s - 1], y_dev(s))

    def small(i):
        return pl.ds(mult(i // 2 * 16, 16), 16), pl.ds(mult(lax.rem(i, 2) * 128, 128), 128)

    def zy_copy(p, s):
        r, c = small(lax.rem(y + s, NY))
        return remote(z_part.at[p, r, c], zy_in.at[p, s - 1], zy_s.at[p, s - 1], zy_r.at[p, s - 1], y_dev(s))

    def yz_copy(p, s):
        r, c = small(lax.rem(z + s, NZ))
        return remote(y_part.at[p, r, c], yz_in.at[p, s - 1], yz_s.at[p, s - 1], yz_r.at[p, s - 1], z_dev(s))

    def z_place(p):
        return gw_out.at[core, pl.ds(mult(z * 32, 32), 32), pl.ds(p * COLS, COLS)]

    def y_place(p):
        return gw_out.at[core, pl.ds(mult(256 + y * 64, 64), 64), pl.ds(p * COLS, COLS)]

    def zy_place(p):
        r = pl.ds(mult(z * 32 + y // 2 * 16, 16), 16)
        return gw_out.at[core, r, pl.ds(mult(p * COLS + lax.rem(y, 2) * 128, 128), 128)]

    def yz_place(p):
        r = pl.ds(mult(256 + y * 64 + z // 2 * 16, 16), 16)
        return gw_out.at[core, r, pl.ds(mult(p * COLS + lax.rem(z, 2) * 128, 128), 128)]

    def zyg_copy(p, s):
        return remote(zy_place(p), zy_place(p), zyg_s.at[p, s - 1], zyg_r.at[p, s - 1], y_dev(s))

    def yzg_copy(p, s):
        return remote(yz_place(p), yz_place(p), yzg_s.at[p, s - 1], yzg_r.at[p, s - 1], z_dev(s))

    def zg_copy(p, s):
        return remote(z_place(p), z_place(p), zg_s.at[p, s - 1], zg_r.at[p, s - 1], z_dev(s))

    def yg_copy(p, s):
        return remote(y_place(p), y_place(p), yg_s.at[p, s - 1], yg_r.at[p, s - 1], y_dev(s))

    def pairg_copy(p):
        block = gw_out.at[core, :, pl.ds(p * COLS, COLS)]
        return remote(block, block, pairg_s.at[p], pairg_r.at[p], {"ctx": partner})

    def stage_a(p):
        pair_copy(p).wait_recv()
        half[p] = (f32(part[p, core]) + f32(pair_in[p])).astype(BF)
        for s in range(1, NZ):
            z_copy(p, s).start()
        for s in range(1, NY):
            y_copy(p, s).start()

    def stage_b(p):
        total = f32(half[p, pl.ds(mult(z * 32, 32), 32), :])
        for s in range(1, NZ):
            z_copy(p, s).wait_recv()
            total += f32(z_in[p, s - 1])
        z_part[p] = total.astype(BF)
        for s in range(1, NY):
            zy_copy(p, s).start()
        total = f32(half[p, pl.ds(mult(256 + y * 64, 64), 64), :])
        for s in range(1, NY):
            y_copy(p, s).wait_recv()
            total += f32(y_in[p, s - 1])
        y_part[p] = total.astype(BF)
        for s in range(1, NZ):
            yz_copy(p, s).start()

    def stage_c(p):
        r, c = small(y)
        total = f32(z_part[p, r, c])
        for s in range(1, NY):
            zy_copy(p, s).wait_recv()
            total += f32(zy_in[p, s - 1])
        zy_place(p)[...] = total.astype(BF)
        for s in range(1, NY):
            zyg_copy(p, s).start()
        r, c = small(z)
        total = f32(y_part[p, r, c])
        for s in range(1, NZ):
            yz_copy(p, s).wait_recv()
            total += f32(yz_in[p, s - 1])
        yz_place(p)[...] = total.astype(BF)
        for s in range(1, NZ):
            yzg_copy(p, s).start()

    def stage_d(p):
        for s in range(1, NY):
            zyg_copy(p, s).wait_recv()
        for s in range(1, NZ):
            zg_copy(p, s).start()
        for s in range(1, NZ):
            yzg_copy(p, s).wait_recv()
        for s in range(1, NY):
            yg_copy(p, s).start()

    def stage_e(p):
        for s in range(1, NZ):
            zg_copy(p, s).wait_recv()
        for s in range(1, NY):
            yg_copy(p, s).wait_recv()
        pairg_copy(p).start()

    def x_copy(s):
        there = lax.rem(x + s, n_head // 2)
        return remote(
            glb.at[pl.ds(mult(there * 2 * rows, 16), 2 * rows)],
            x_in.at[s - 1],
            x_s.at[s - 1],
            x_r.at[s - 1],
            {"head": there * 2 + y_lo},
        )

    def yl_copy():
        return remote(
            x_part.at[pl.ds(mult((1 - y_lo) * rows, 16), rows)],
            yl_in,
            yl_s,
            yl_r,
            {"head": head + 1 - 2 * y_lo},
        )

    def ctx_copy(s):
        return remote(
            ctx_part.at[:, slot_cols(PREV - s)],
            ctx_in.at[s - 1],
            ctx_s.at[s - 1],
            ctx_r.at[s - 1],
            {"ctx": me - s},
        )

    def headg_copy(s):
        block = gl_out.at[head_rows]
        return remote(block, block, headg_s.at[s - 1], headg_r.at[s - 1], {"head": at_head(s)})

    def latent_terms():
        glb[pl.ds(0, LAT), :] = nn(wcat[...], dcat[...]).astype(BF)
        glb[pl.ds(LAT, ROPE), :] = rope_sum[...].astype(BF)
        glb[pl.ds(LAT + ROPE, glb.shape[0] - LAT - ROPE), :] = jnp.zeros(
            (glb.shape[0] - LAT - ROPE, WIN), BF
        )
        for s in range(1, n_head // 2):
            x_copy(s).start()

    def latent_x():
        total = f32(glb[pl.ds(mult(x * 2 * rows, 16), 2 * rows), :])
        for s in range(1, n_head // 2):
            x_copy(s).wait_recv()
            total += f32(x_in[s - 1])
        x_part[...] = total.astype(BF)
        yl_copy().start()

    def latent_y():
        yl_copy().wait_recv()
        total = f32(x_part[pl.ds(mult(y_lo * rows, 16), rows), :]) + f32(yl_in[...])
        ctx_part[...] = total.astype(BF)
        for s in range(1, PREV + 1):

            @pl.when(me >= s)
            def _():
                ctx_copy(s).start()

    def latent_blocks():
        for s in range(1, PREV + 1):

            @pl.when(me + s < n_ctx)
            def _():
                ctx_copy(s).wait_recv()

            @pl.when(me + s >= n_ctx)
            def _():
                ctx_in[s - 1] = jnp.zeros(ctx_in.shape[1:], BF)

        total = f32(ctx_part[:, slot_cols(PREV)])
        for s in range(1, PREV + 1):
            total += f32(ctx_in[s - 1])
        gl_out[head_rows, :] = total.astype(BF)
        for s in range(1, n_head):
            headg_copy(s).start()

    one_head(0)
    one_head(1)
    weight_terms(0)
    one_head(2)
    stage_a(0)
    one_head(3)
    latent_terms()
    weight_terms(1)
    stage_a(1)
    stage_b(0)
    stage_b(1)
    stage_c(0)
    latent_x()
    stage_c(1)
    stage_d(0)
    latent_y()
    stage_d(1)
    latent_blocks()
    stage_e(0)
    stage_e(1)

    @pl.when(me + 4 < n_ctx)
    def _():
        far.wait_send()

    @pl.when(me + 2 < n_ctx)
    def _():
        near.wait_send()

    for i in range(2):
        mate_copy(i, PREV).wait_send()

    @pl.when(me >= 4)
    def _():
        for s in range(1, n_head):
            far_copy(s).wait_send()

    for s in range(1, n_head // 2):
        x_copy(s).wait_send()
    yl_copy().wait_send()
    for s in range(1, n_head):
        headg_copy(s).wait()
    for s in range(1, PREV + 1):

        @pl.when(me >= s)
        def _():
            ctx_copy(s).wait_send()

    for p in range(PIECES):
        pair_copy(p).wait_send()
        for s in range(1, NZ):
            z_copy(p, s).wait_send()
            yz_copy(p, s).wait_send()
            yzg_copy(p, s).wait_send()
            zg_copy(p, s).wait_send()
        for s in range(1, NY):
            y_copy(p, s).wait_send()
            zy_copy(p, s).wait_send()
            zyg_copy(p, s).wait_send()
            yg_copy(p, s).wait_send()
        pairg_copy(p).wait()


def write_out(attn, gq, gl, gw, attn_out, gq_out, gl_out, gk_out, gv_out, *rest):
    stages, load_sem, store_sem = rest[:5], rest[5], rest[6]
    pairs = [
        (gw.at[0], gk_out),
        (gw.at[1], gv_out),
        (gq, gq_out),
        (gl.at[pl.ds(0, LAT + ROPE)], gl_out),
        (attn, attn_out),
    ]
    loads = [
        pltpu.make_async_copy(src, stage, load_sem.at[i])
        for i, ((src, _), stage) in enumerate(zip(pairs, stages))
    ]
    stores = [
        pltpu.make_async_copy(stage, dst, store_sem.at[i])
        for i, ((_, dst), stage) in enumerate(zip(pairs, stages))
    ]
    for load in loads:
        load.start()
    for load, store in zip(loads, stores):
        load.wait()
        store.start()
    for store in stores:
        store.wait()


def per_device(queries, latent, w_key, w_value, grad_out, segment_ids):
    n_ctx = lax.axis_size("ctx")
    n_head = lax.axis_size("head")
    vmem = pl.BlockSpec(memory_space=pltpu.VMEM)
    hbm = pl.BlockSpec(memory_space=pltpu.HBM)
    dma = pltpu.SemaphoreType.DMA
    rows = 80

    def buf(*shape, dtype=BF):
        return pltpu.VMEM(shape, dtype)

    def sems(*shape):
        return [dma(shape), dma(shape)]

    attn_out, grad_queries, grad_latent, grad_w = pl.pallas_call(
        functools.partial(kernel, n_ctx, n_head),
        out_shape=[
            jax.ShapeDtypeStruct((TOK, HEADS * VDIM), BF),
            jax.ShapeDtypeStruct((TOK, HEADS * QK), BF),
            jax.ShapeDtypeStruct((rows * n_head, TOK), BF),
            jax.ShapeDtypeStruct((2, LAT, HEADS * NOPE), BF),
        ],
        in_specs=[hbm] * 6,
        out_specs=[vmem] * 4,
        scratch_shapes=[
            buf(TOK, HEADS * QK),
            buf(LAT, 2 * HEADS * NOPE),
            buf(TOK, HEADS * VDIM),
            buf(n_ctx, TOK, dtype=jnp.int32),
            buf(rows * n_head, WIN),
            buf(2 * HEADS * NOPE, LAT),
            buf(HEADS, TOK, QK),
            buf(HEADS, QK, TOK),
            buf(HEADS, VDIM, TOK),
            buf(HEADS, QK, WIN),
            buf(HEADS, VDIM, WIN),
            buf(TOK, WIN, dtype=jnp.float32),
            buf(2 * HEADS * NOPE, WIN),
            buf(ROPE, WIN, dtype=jnp.float32),
            buf(PIECES, 2, LAT, COLS),
            buf(PIECES, LAT, COLS),
            buf(PIECES, LAT, COLS),
            buf(PIECES, NZ - 1, 32, COLS),
            buf(PIECES, NY - 1, 64, COLS),
            buf(PIECES, NY - 1, 16, 128),
            buf(PIECES, NZ - 1, 16, 128),
            buf(PIECES, 32, COLS),
            buf(PIECES, 64, COLS),
            buf(rows * n_head, WIN),
            buf(n_head // 2 - 1, 2 * rows, WIN),
            buf(2 * rows, WIN),
            buf(rows, WIN),
            buf(rows, WIN),
            buf(PREV, rows, TOK),
            dma((4 + 2 * PIECES,)),
            *sems(2),
            *sems(n_head - 1),
            *sems(2),
            *sems(PIECES),
            *sems(PIECES, NZ - 1),
            *sems(PIECES, NY - 1),
            *sems(PIECES, NY - 1),
            *sems(PIECES, NZ - 1),
            *sems(PIECES, NY - 1),
            *sems(PIECES, NZ - 1),
            *sems(PIECES, NZ - 1),
            *sems(PIECES, NY - 1),
            *sems(PIECES),
            *sems(n_head // 2 - 1),
            dma,
            dma,
            *sems(PREV),
            *sems(n_head - 1),
        ],
        compiler_params=pltpu.CompilerParams(
            collective_id=0, has_side_effects=True, vmem_limit_bytes=60 * 2**20
        ),
        name="attention",
    )(queries, latent.T, w_key, w_value, grad_out, segment_ids.reshape(n_ctx, TOK))
    any_space = pl.BlockSpec(memory_space=pl.ANY)
    attn_out, grad_queries, grad_latent, grad_w_key, grad_w_value = pl.pallas_call(
        write_out,
        out_shape=[
            jax.ShapeDtypeStruct((TOK, HEADS * VDIM), BF),
            jax.ShapeDtypeStruct((TOK, HEADS * QK), BF),
            jax.ShapeDtypeStruct((LAT + ROPE, TOK), BF),
            jax.ShapeDtypeStruct((LAT, HEADS * NOPE), BF),
            jax.ShapeDtypeStruct((LAT, HEADS * NOPE), BF),
        ],
        in_specs=[any_space] * 4,
        out_specs=[hbm] * 5,
        scratch_shapes=[
            buf(LAT, HEADS * NOPE),
            buf(LAT, HEADS * NOPE),
            buf(TOK, HEADS * QK),
            buf(LAT + ROPE, TOK),
            buf(TOK, HEADS * VDIM),
            *sems(5),
        ],
        compiler_params=pltpu.CompilerParams(vmem_limit_bytes=60 * 2**20),
        name="write_out",
    )(attn_out, grad_queries, grad_latent, grad_w)
    return (attn_out, grad_queries, grad_latent.T, grad_w_key, grad_w_value)


def solution(mesh):
    return jax.shard_map(
        per_device,
        mesh=mesh,
        in_specs=(
            P("ctx", "head"),
            P("ctx", None),
            P(None, "head"),
            P(None, "head"),
            P("ctx", "head"),
            P(),
        ),
        out_specs=(
            P("ctx", "head"),
            P("ctx", "head"),
            P("ctx", None),
            P(None, "head"),
            P(None, "head"),
        ),
        check_vma=False,
    )
```

```python
import functools
import math

import jax
import jax.numpy as jnp
from jax import lax
from jax.experimental import pallas as pl
from jax.experimental.pallas import tpu as pltpu
from jax.sharding import PartitionSpec as P

LAT = 512
ROPE = 64
NOPE = 128
VDIM = 128
PREV = 4
NZ = 8
NY = 4
TOK = 128
WIN = (PREV + 1) * TOK
QK = NOPE + ROPE
HEADS = 4
PIECES = 2
COLS = HEADS // PIECES * NOPE
MESH = pl.DeviceIdType.MESH
BF = jnp.bfloat16
SCALE = 1.0 / math.sqrt(QK)


def f32(x):
    return x.astype(jnp.float32)


def nn(a, b):
    return jnp.dot(a, b, preferred_element_type=jnp.float32)


def nt(a, b):
    return lax.dot_general(a, b, (((1,), (1,)), ((), ())), preferred_element_type=jnp.float32)


def mult(x, m):
    return pl.multiple_of(x, m)


def slot_cols(slot):
    return pl.ds(slot * TOK, TOK)


def kernel(n_ctx, n_head, *refs):
    (
        q_hbm,
        lat_hbm,
        wk_hbm,
        wv_hbm,
        do_hbm,
        seg_hbm,
        attn_ref,
        gq_ref,
        gl_out,
        gw_out,
        q_ref,
        wcat,
        do_ref,
        seg_ref,
        win,
        wt,
        qs,
        qt,
        dot,
        kt,
        vt,
        bias,
        dcat,
        rope_sum,
        part,
        pair_in,
        half,
        z_in,
        y_in,
        zy_in,
        yz_in,
        z_part,
        y_part,
        glb,
        x_in,
        x_part,
        yl_in,
        ctx_part,
        ctx_in,
        load_sem,
        halo_s,
        halo_r,
        far_s,
        far_r,
        mate_s,
        mate_r,
        pair_s,
        pair_r,
        z_s,
        z_r,
        y_s,
        y_r,
        zy_s,
        zy_r,
        yz_s,
        yz_r,
        zyg_s,
        zyg_r,
        yzg_s,
        yzg_r,
        zg_s,
        zg_r,
        yg_s,
        yg_r,
        pairg_s,
        pairg_r,
        x_s,
        x_r,
        yl_s,
        yl_r,
        ctx_s,
        ctx_r,
        headg_s,
        headg_r,
    ) = refs
    me = lax.axis_index("ctx")
    head = lax.axis_index("head")
    core = lax.rem(me, 2)
    z = lax.rem(me // 2, NZ)
    y = me // (2 * NZ)
    partner = me + 1 - 2 * core
    rows = glb.shape[0] // n_head
    x = head // 2
    y_lo = lax.rem(head, 2)
    head_rows = pl.ds(mult(head * rows, 16), rows)

    def z_dev(s):
        return {"ctx": (y * NZ + lax.rem(z + s, NZ)) * 2 + core}

    def y_dev(s):
        return {"ctx": (lax.rem(y + s, NY) * NZ + z) * 2 + core}

    def at_head(s):
        return lax.rem(head + s, n_head)

    def remote(src, dst, send, recv, device):
        return pltpu.make_async_remote_copy(
            src_ref=src, dst_ref=dst, send_sem=send, recv_sem=recv, device_id=device, device_id_type=MESH
        )

    def phase(block, send, recv):
        return remote(block, block, send, recv, {"ctx": partner})

    pad = pl.ds(LAT + ROPE, win.shape[0] - LAT - ROPE)
    win[pad, slot_cols(PREV)] = jnp.zeros((win.shape[0] - LAT - ROPE, TOK), BF)
    live = pl.ds(0, LAT + ROPE)
    own_block = win.at[live, slot_cols(PREV)]
    loads = [
        pltpu.make_async_copy(src, dst, load_sem.at[i])
        for i, (src, dst) in enumerate(
            [(lat_hbm, own_block), (seg_hbm, seg_ref), (q_hbm, q_ref), (do_hbm, do_ref)]
            + [
                (w.at[:, pl.ds(p * COLS, COLS)], wcat.at[:, pl.ds((2 * p + kind) * COLS, COLS)])
                for p in range(PIECES)
                for kind, w in enumerate((wk_hbm, wv_hbm))
            ]
        )
    ]
    for load in loads:
        load.start()

    barrier = pltpu.get_barrier_semaphore()

    def greet(device):
        pl.semaphore_signal(barrier, inc=1, device_id=device, device_id_type=MESH)

    for s in range(1, PREV + 1):

        @pl.when(me >= s)
        def _():
            greet({"ctx": me - s})

        @pl.when(me + s < n_ctx)
        def _():
            greet({"ctx": me + s})

    greet({"ctx": partner})
    for s in range(1, NZ):
        greet(z_dev(s))
    for s in range(1, NY):
        greet(y_dev(s))
    for s in range(1, n_head):
        greet({"head": at_head(s)})
    pl.semaphore_wait(
        barrier,
        NZ - 1 + NY - 1 + n_head + jnp.minimum(me, PREV) + jnp.minimum(n_ctx - 1 - me, PREV),
    )

    near = remote(
        own_block, win.at[live, slot_cols(2)], halo_s.at[0], halo_r.at[0], {"ctx": me + 2}
    )
    far = remote(
        win.at[head_rows, slot_cols(PREV)],
        win.at[head_rows, slot_cols(0)],
        halo_s.at[1],
        halo_r.at[1],
        {"ctx": me + 4},
    )

    def far_copy(s):
        block = win.at[head_rows, slot_cols(0)]
        return remote(block, block, far_s, far_r, {"head": at_head(s)})

    def mate_copy(i, src):
        return remote(
            win.at[live, slot_cols(src)],
            win.at[live, slot_cols(PREV - 1 - 2 * i)],
            mate_s.at[i],
            mate_r.at[i],
            {"ctx": partner},
        )

    loads[0].wait()

    @pl.when(me + 4 < n_ctx)
    def _():
        far.start()

    @pl.when(me + 2 < n_ctx)
    def _():
        near.start()

    @pl.when(core == 0)
    def _():
        mate_copy(0, PREV).start()

    far_all = phase(win.at[pl.ds(0, (n_head - 1) * rows), slot_cols(0)], far_s, far_r)

    for load in loads[1:]:
        load.wait()
    for h in range(HEADS):
        block = q_ref[:, pl.ds(h * QK, QK)]
        qs[h] = block
        qt[h] = block.T
        dot[h] = do_ref[:, pl.ds(h * VDIM, VDIM)].T
    own = seg_ref[pl.ds(me, 1), :]
    query_seg = jnp.broadcast_to(own, (TOK, TOK)).T
    for s in range(PREV + 1):
        place = me - PREV + s
        key_seg = jnp.where(place >= 0, seg_ref[pl.ds(jnp.maximum(place, 0), 1), :], -1)
        allowed = query_seg == key_seg
        if s == PREV:
            allowed &= lax.broadcasted_iota(jnp.int32, (TOK, TOK), 1) <= lax.broadcasted_iota(
                jnp.int32, (TOK, TOK), 0
            )
        bias[:, slot_cols(s)] = jnp.where(allowed, 0.0, -jnp.inf)

    @pl.when(me >= 4)
    def _():
        far.wait_recv()
        for s in range(1, n_head):
            far_copy(s).start()

    for i in range(2 * PIECES):
        wt[pl.ds(i * COLS, COLS), :] = wcat[:, pl.ds(i * COLS, COLS)].T
    def project(start, size):
        cols = pl.ds(start, size)
        each = HEADS // PIECES
        for p in range(PIECES):
            made = nn(wt[pl.ds(2 * p * COLS, 2 * COLS), :], win[pl.ds(0, LAT), cols]).astype(BF)
            for j in range(each):
                kt[p * each + j, pl.ds(0, NOPE), cols] = made[j * NOPE : (j + 1) * NOPE]
                vt[p * each + j, :, cols] = made[COLS + j * VDIM : COLS + (j + 1) * VDIM]
        for h in range(HEADS):
            kt[h, pl.ds(NOPE, ROPE), cols] = win[pl.ds(LAT, ROPE), cols]

    project(PREV * TOK, TOK)

    @pl.when(me >= 2)
    def _():
        near.wait_recv()

    @pl.when(me < 2)
    def _():
        win[live, slot_cols(2)] = jnp.zeros((LAT + ROPE, TOK), BF)

    @pl.when(core == 0)
    def _():
        mate_copy(1, 2).start()

    @pl.when(core == 1)
    def _():
        mate_copy(0, 2).start()

    mate_copy(0, PREV).wait_recv()
    project(2 * TOK, 2 * TOK)

    @pl.when(me >= 4)
    def _():
        far_all.wait_recv()

    @pl.when(me < 4)
    def _():
        win[live, slot_cols(0)] = jnp.zeros((LAT + ROPE, TOK), BF)

    @pl.when(core == 1)
    def _():
        mate_copy(1, 0).start()

    @pl.when(me + 4 < n_ctx)
    def _():
        far.wait_send()

    @pl.when(me + 2 < n_ctx)
    def _():
        near.wait_send()

    mate_copy(1, PREV).wait_recv()
    project(0, 2 * TOK)

    for i in range(2):
        mate_copy(i, PREV).wait_send()

    @pl.when(me >= 4)
    def _():
        far_all.wait_send()

    def one_head(h):
        p, j = divmod(h, HEADS // PIECES)
        base = 2 * p * COLS + j * NOPE
        scores = nn(qs[h], kt[h]) * SCALE + bias[...]
        expo = jnp.exp(scores - jnp.max(scores, axis=1, keepdims=True))
        scaling = 1.0 / jnp.sum(expo, axis=1, keepdims=True)
        out = (nt(expo.astype(BF), vt[h]) * scaling).astype(BF)
        attn_ref[:, pl.ds(h * VDIM, VDIM)] = out
        upstream = do_ref[:, pl.ds(h * VDIM, VDIM)]
        delta = jnp.sum(f32(upstream) * f32(out), axis=1, keepdims=True)
        probs = expo * scaling
        grad_scores = (probs * (nn(upstream, vt[h]) - delta)).astype(BF)
        gq_ref[:, pl.ds(h * QK, QK)] = (nt(grad_scores, kt[h]) * SCALE).astype(BF)
        term = (nn(qt[h], grad_scores) * SCALE).astype(BF)
        dcat[pl.ds(base, NOPE), :] = term[:NOPE]
        rope_sum[...] = f32(term[NOPE:]) if h == 0 else rope_sum[...] + f32(term[NOPE:])
        dcat[pl.ds(base + COLS, VDIM), :] = nn(dot[h], probs.astype(BF)).astype(BF)

    def pair_copy(p):
        return remote(
            part.at[p, 1 - core], pair_in.at[p], pair_s.at[p], pair_r.at[p], {"ctx": partner}
        )

    def weight_terms(p):
        terms = nt(win[pl.ds(0, LAT), :], dcat[pl.ds(2 * p * COLS, 2 * COLS), :]).astype(BF)
        part[p, 0] = terms[:, :COLS]
        part[p, 1] = terms[:, COLS:]
        pair_copy(p).start()

    def z_copy(p, s):
        block = pl.ds(mult(lax.rem(z + s, NZ) * 32, 32), 32)
        return remote(half.at[p, block], z_in.at[p, s - 1], z_s.at[p], z_r.at[p], z_dev(s))

    def y_copy(p, s):
        block = pl.ds(mult(256 + lax.rem(y + s, NY) * 64, 64), 64)
        return remote(half.at[p, block], y_in.at[p, s - 1], y_s.at[p], y_r.at[p], y_dev(s))

    def small(i):
        return pl.ds(mult(i // 2 * 16, 16), 16), pl.ds(mult(lax.rem(i, 2) * (COLS // 2), 128), COLS // 2)

    def zy_copy(p, s):
        r, c = small(lax.rem(y + s, NY))
        return remote(z_part.at[p, r, c], zy_in.at[p, s - 1], zy_s.at[p], zy_r.at[p], y_dev(s))

    def yz_copy(p, s):
        r, c = small(lax.rem(z + s, NZ))
        return remote(y_part.at[p, r, c], yz_in.at[p, s - 1], yz_s.at[p], yz_r.at[p], z_dev(s))

    def z_place(p):
        return gw_out.at[core, pl.ds(mult(z * 32, 32), 32), pl.ds(p * COLS, COLS)]

    def y_place(p):
        return gw_out.at[core, pl.ds(mult(256 + y * 64, 64), 64), pl.ds(p * COLS, COLS)]

    def zy_place(p):
        r = pl.ds(mult(z * 32 + y // 2 * 16, 16), 16)
        return gw_out.at[core, r, pl.ds(mult(p * COLS + lax.rem(y, 2) * (COLS // 2), 128), COLS // 2)]

    def yz_place(p):
        r = pl.ds(mult(256 + y * 64 + z // 2 * 16, 16), 16)
        return gw_out.at[core, r, pl.ds(mult(p * COLS + lax.rem(z, 2) * (COLS // 2), 128), COLS // 2)]

    def zyg_copy(p, s):
        return remote(zy_place(p), zy_place(p), zyg_s.at[p], zyg_r.at[p], y_dev(s))

    def yzg_copy(p, s):
        return remote(yz_place(p), yz_place(p), yzg_s.at[p], yzg_r.at[p], z_dev(s))

    def zg_copy(p, s):
        return remote(z_place(p), z_place(p), zg_s.at[p], zg_r.at[p], z_dev(s))

    def yg_copy(p, s):
        return remote(y_place(p), y_place(p), yg_s.at[p], yg_r.at[p], y_dev(s))

    def pairg_copy(p):
        block = gw_out.at[core, :, pl.ds(p * COLS, COLS)]
        return remote(block, block, pairg_s.at[p], pairg_r.at[p], {"ctx": partner})

    def z_phase(p):
        return phase(z_in.at[p], z_s.at[p], z_r.at[p])

    def y_phase(p):
        return phase(y_in.at[p], y_s.at[p], y_r.at[p])

    def zy_phase(p):
        return phase(zy_in.at[p], zy_s.at[p], zy_r.at[p])

    def yz_phase(p):
        return phase(yz_in.at[p], yz_s.at[p], yz_r.at[p])

    def zyg_phase(p):
        return phase(zy_in.at[p], zyg_s.at[p], zyg_r.at[p])

    def yzg_phase(p):
        return phase(yz_in.at[p], yzg_s.at[p], yzg_r.at[p])

    def zg_phase(p):
        return phase(z_in.at[p], zg_s.at[p], zg_r.at[p])

    def yg_phase(p):
        return phase(y_in.at[p], yg_s.at[p], yg_r.at[p])

    def stage_a(p):
        pair_copy(p).wait_recv()
        half[p] = (f32(part[p, core]) + f32(pair_in[p])).astype(BF)
        for s in range(1, NZ):
            z_copy(p, s).start()
        for s in range(1, NY):
            y_copy(p, s).start()
        pair_copy(p).wait_send()

    def stage_b(p):
        z_phase(p).wait_recv()
        total = f32(half[p, pl.ds(mult(z * 32, 32), 32), :])
        for s in range(1, NZ):
            total += f32(z_in[p, s - 1])
        z_part[p] = total.astype(BF)
        for s in range(1, NY):
            zy_copy(p, s).start()
        y_phase(p).wait_recv()
        total = f32(half[p, pl.ds(mult(256 + y * 64, 64), 64), :])
        for s in range(1, NY):
            total += f32(y_in[p, s - 1])
        y_part[p] = total.astype(BF)
        for s in range(1, NZ):
            yz_copy(p, s).start()
        z_phase(p).wait_send()
        y_phase(p).wait_send()

    def stage_c(p):
        zy_phase(p).wait_recv()
        r, c = small(y)
        total = f32(z_part[p, r, c])
        for s in range(1, NY):
            total += f32(zy_in[p, s - 1])
        zy_place(p)[...] = total.astype(BF)
        for s in range(1, NY):
            zyg_copy(p, s).start()
        yz_phase(p).wait_recv()
        r, c = small(z)
        total = f32(y_part[p, r, c])
        for s in range(1, NZ):
            total += f32(yz_in[p, s - 1])
        yz_place(p)[...] = total.astype(BF)
        for s in range(1, NZ):
            yzg_copy(p, s).start()
        zy_phase(p).wait_send()
        yz_phase(p).wait_send()

    def stage_d(p):
        zyg_phase(p).wait_recv()
        for s in range(1, NZ):
            zg_copy(p, s).start()
        yzg_phase(p).wait_recv()
        for s in range(1, NY):
            yg_copy(p, s).start()
        zyg_phase(p).wait_send()
        yzg_phase(p).wait_send()

    def stage_e(p):
        zg_phase(p).wait_recv()
        yg_phase(p).wait_recv()
        pairg_copy(p).start()
        zg_phase(p).wait_send()
        yg_phase(p).wait_send()

    def x_copy(s):
        there = lax.rem(x + s, n_head // 2)
        return remote(
            glb.at[pl.ds(mult(there * 2 * rows, 16), 2 * rows)],
            x_in.at[s - 1],
            x_s,
            x_r,
            {"head": there * 2 + y_lo},
        )

    def yl_copy():
        return remote(
            x_part.at[pl.ds(mult((1 - y_lo) * rows, 16), rows)],
            yl_in,
            yl_s,
            yl_r,
            {"head": head + 1 - 2 * y_lo},
        )

    def ctx_copy(s):
        return remote(
            ctx_part.at[:, slot_cols(PREV - s)],
            ctx_in.at[s - 1],
            ctx_s.at[s - 1],
            ctx_r.at[s - 1],
            {"ctx": me - s},
        )

    def headg_copy(s):
        block = gl_out.at[head_rows]
        return remote(block, block, headg_s, headg_r, {"head": at_head(s)})

    def latent_terms():
        glb[pl.ds(0, LAT), :] = nn(wcat[...], dcat[...]).astype(BF)
        glb[pl.ds(LAT, ROPE), :] = rope_sum[...].astype(BF)
        glb[pl.ds(LAT + ROPE, glb.shape[0] - LAT - ROPE), :] = jnp.zeros(
            (glb.shape[0] - LAT - ROPE, WIN), BF
        )
        for s in range(1, n_head // 2):
            x_copy(s).start()

    def latent_x():
        phase(x_in, x_s, x_r).wait_recv()
        total = f32(glb[pl.ds(mult(x * 2 * rows, 16), 2 * rows), :])
        for s in range(1, n_head // 2):
            total += f32(x_in[s - 1])
        x_part[...] = total.astype(BF)
        yl_copy().start()
        phase(x_in, x_s, x_r).wait_send()

    def latent_y():
        yl_copy().wait_recv()
        total = f32(x_part[pl.ds(mult(y_lo * rows, 16), rows), :]) + f32(yl_in[...])
        ctx_part[...] = total.astype(BF)
        for s in range(1, PREV + 1):

            @pl.when(me >= s)
            def _():
                ctx_copy(s).start()

        yl_copy().wait_send()

    def latent_blocks():
        for s in range(1, PREV + 1):

            @pl.when(me + s < n_ctx)
            def _():
                ctx_copy(s).wait_recv()

            @pl.when(me + s >= n_ctx)
            def _():
                ctx_in[s - 1] = jnp.zeros(ctx_in.shape[1:], BF)

        total = f32(ctx_part[:, slot_cols(PREV)])
        for s in range(1, PREV + 1):
            total += f32(ctx_in[s - 1])
        gl_out[head_rows, :] = total.astype(BF)
        for s in range(1, n_head):
            headg_copy(s).start()

    one_head(0)
    one_head(1)
    weight_terms(0)
    one_head(2)
    stage_a(0)
    one_head(3)
    weight_terms(1)
    latent_terms()
    stage_a(1)
    stage_b(0)
    stage_b(1)
    stage_c(0)
    stage_c(1)
    latent_x()
    stage_d(0)
    stage_d(1)
    latent_y()
    stage_e(0)
    latent_blocks()
    stage_e(1)

    for s in range(1, PREV + 1):

        @pl.when(me >= s)
        def _():
            ctx_copy(s).wait_send()

    phase(gl_out.at[pl.ds(0, (n_head - 1) * rows)], headg_s, headg_r).wait()
    for p in range(PIECES):
        pairg_copy(p).wait()


def write_out(attn, gq, gl, gw, attn_out, gq_out, gl_out, gk_out, gv_out, *rest):
    stages, load_sem, store_sem = rest[:5], rest[5], rest[6]
    pairs = [
        (gw.at[0], gk_out),
        (gw.at[1], gv_out),
        (gq, gq_out),
        (gl.at[pl.ds(0, LAT + ROPE)], gl_out),
        (attn, attn_out),
    ]
    loads = [
        pltpu.make_async_copy(src, stage, load_sem.at[i])
        for i, ((src, _), stage) in enumerate(zip(pairs, stages))
    ]
    stores = [
        pltpu.make_async_copy(stage, dst, store_sem.at[i])
        for i, ((_, dst), stage) in enumerate(zip(pairs, stages))
    ]
    for load in loads:
        load.start()
    for load, store in zip(loads, stores):
        load.wait()
        store.start()
    for store in stores:
        store.wait()


def per_device(queries, latent, w_key, w_value, grad_out, segment_ids):
    n_ctx = lax.axis_size("ctx")
    n_head = lax.axis_size("head")
    vmem = pl.BlockSpec(memory_space=pltpu.VMEM)
    hbm = pl.BlockSpec(memory_space=pltpu.HBM)
    dma = pltpu.SemaphoreType.DMA
    rows = 80

    def buf(*shape, dtype=BF):
        return pltpu.VMEM(shape, dtype)

    def sems(*shape):
        return [dma(shape), dma(shape)]

    attn_out, grad_queries, grad_latent, grad_w = pl.pallas_call(
        functools.partial(kernel, n_ctx, n_head),
        out_shape=[
            jax.ShapeDtypeStruct((TOK, HEADS * VDIM), BF),
            jax.ShapeDtypeStruct((TOK, HEADS * QK), BF),
            jax.ShapeDtypeStruct((rows * n_head, TOK), BF),
            jax.ShapeDtypeStruct((2, LAT, HEADS * NOPE), BF),
        ],
        in_specs=[hbm] * 6,
        out_specs=[vmem] * 4,
        scratch_shapes=[
            buf(TOK, HEADS * QK),
            buf(LAT, 2 * HEADS * NOPE),
            buf(TOK, HEADS * VDIM),
            buf(n_ctx, TOK, dtype=jnp.int32),
            buf(rows * n_head, WIN),
            buf(2 * HEADS * NOPE, LAT),
            buf(HEADS, TOK, QK),
            buf(HEADS, QK, TOK),
            buf(HEADS, VDIM, TOK),
            buf(HEADS, QK, WIN),
            buf(HEADS, VDIM, WIN),
            buf(TOK, WIN, dtype=jnp.float32),
            buf(2 * HEADS * NOPE, WIN),
            buf(ROPE, WIN, dtype=jnp.float32),
            buf(PIECES, 2, LAT, COLS),
            buf(PIECES, LAT, COLS),
            buf(PIECES, LAT, COLS),
            buf(PIECES, NZ - 1, 32, COLS),
            buf(PIECES, NY - 1, 64, COLS),
            buf(PIECES, NY - 1, 16, COLS // 2),
            buf(PIECES, NZ - 1, 16, COLS // 2),
            buf(PIECES, 32, COLS),
            buf(PIECES, 64, COLS),
            buf(rows * n_head, WIN),
            buf(n_head // 2 - 1, 2 * rows, WIN),
            buf(2 * rows, WIN),
            buf(rows, WIN),
            buf(rows, WIN),
            buf(PREV, rows, TOK),
            dma((4 + 2 * PIECES,)),
            *sems(2),
            dma,
            dma,
            *sems(2),
            *sems(PIECES),
            *sems(PIECES),
            *sems(PIECES),
            *sems(PIECES),
            *sems(PIECES),
            *sems(PIECES),
            *sems(PIECES),
            *sems(PIECES),
            *sems(PIECES),
            *sems(PIECES),
            dma,
            dma,
            dma,
            dma,
            *sems(PREV),
            dma,
            dma,
        ],
        compiler_params=pltpu.CompilerParams(
            collective_id=0, has_side_effects=True, vmem_limit_bytes=60 * 2**20
        ),
        name="attention",
    )(queries, latent.T, w_key, w_value, grad_out, segment_ids.reshape(n_ctx, TOK))
    any_space = pl.BlockSpec(memory_space=pl.ANY)
    attn_out, grad_queries, grad_latent, grad_w_key, grad_w_value = pl.pallas_call(
        write_out,
        out_shape=[
            jax.ShapeDtypeStruct((TOK, HEADS * VDIM), BF),
            jax.ShapeDtypeStruct((TOK, HEADS * QK), BF),
            jax.ShapeDtypeStruct((LAT + ROPE, TOK), BF),
            jax.ShapeDtypeStruct((LAT, HEADS * NOPE), BF),
            jax.ShapeDtypeStruct((LAT, HEADS * NOPE), BF),
        ],
        in_specs=[any_space] * 4,
        out_specs=[hbm] * 5,
        scratch_shapes=[
            buf(LAT, HEADS * NOPE),
            buf(LAT, HEADS * NOPE),
            buf(TOK, HEADS * QK),
            buf(LAT + ROPE, TOK),
            buf(TOK, HEADS * VDIM),
            *sems(5),
        ],
        compiler_params=pltpu.CompilerParams(vmem_limit_bytes=60 * 2**20),
        name="write_out",
    )(attn_out, grad_queries, grad_latent, grad_w)
    return (attn_out, grad_queries, grad_latent.T, grad_w_key, grad_w_value)


def solution(mesh):
    return jax.shard_map(
        per_device,
        mesh=mesh,
        in_specs=(
            P("ctx", "head"),
            P("ctx", None),
            P(None, "head"),
            P(None, "head"),
            P("ctx", "head"),
            P(),
        ),
        out_specs=(
            P("ctx", "head"),
            P("ctx", "head"),
            P("ctx", None),
            P(None, "head"),
            P(None, "head"),
        ),
        check_vma=False,
    )
```

```python
import functools
import math

import jax
import jax.numpy as jnp
from jax import lax
from jax.experimental import pallas as pl
from jax.experimental.pallas import tpu as pltpu
from jax.sharding import PartitionSpec as P

LAT = 512
ROPE = 64
NOPE = 128
VDIM = 128
PREV = 4
NZ = 8
NY = 4
TOK = 128
WIN = (PREV + 1) * TOK
QK = NOPE + ROPE
HEADS = 4
PIECES = (((0, 1), 256), ((2, 3), 256))
WIDE = [len(heads) * NOPE for heads, _ in PIECES]
FIRST = [heads[0] * NOPE for heads, _ in PIECES]
A_ROWS = [a_rows for _, a_rows in PIECES]
B_ROWS = [512 - a_rows for a_rows in A_ROWS]
FAR_Z = (4, 3, 5, 2, 6, 1, 7)
FAR_Y = (2, 1, 3)
MESH = pl.DeviceIdType.MESH
BF = jnp.bfloat16
SCALE = 1.0 / math.sqrt(QK)


def f32(x):
    return x.astype(jnp.float32)


def nn(a, b):
    return jnp.dot(a, b, preferred_element_type=jnp.float32)


def nt(a, b):
    return lax.dot_general(a, b, (((1,), (1,)), ((), ())), preferred_element_type=jnp.float32)


def mult(x, m):
    return pl.multiple_of(x, m)


def slot_cols(slot):
    return pl.ds(slot * TOK, TOK)


def kernel(n_ctx, n_head, *refs):
    (
        q_hbm,
        lat_hbm,
        wk_hbm,
        wv_hbm,
        do_hbm,
        seg_hbm,
        attn_out,
        gq_out,
        gl_out,
        gw_out,
        attn_ref,
        gq_ref,
        gl_ref,
        gw_ref,
        q_ref,
        wcat,
        do_ref,
        seg_ref,
        win,
        wt,
        qs,
        qt,
        dot,
        kt,
        vt,
        bias,
        raw_scores,
        raw_grads,
        dcat,
        rope_sum,
        *by_piece,
        glb,
        x_in,
        x_part,
        yl_in,
        ctx_part,
        ctx_in,
        load_sem,
        halo_s,
        halo_r,
        far_s,
        far_r,
        mate_s,
        mate_r,
        pair_s,
        pair_r,
        z_s,
        z_r,
        y_s,
        y_r,
        zy_s,
        zy_r,
        yz_s,
        yz_r,
        yzg_s,
        yzg_r,
        zg_s,
        zg_r,
        yg_s,
        yg_r,
        pairg_s,
        pairg_r,
        x_s,
        x_r,
        yl_s,
        yl_r,
        ctx_s,
        ctx_r,
        headg_s,
        headg_r,
        store_sem,
    ) = refs
    part, pair_in, half, z_in, zy_all, y_in, yz_in, y_part = (
        by_piece[i * len(PIECES) : (i + 1) * len(PIECES)] for i in range(8)
    )
    me = lax.axis_index("ctx")
    head = lax.axis_index("head")
    core = lax.rem(me, 2)
    z = lax.rem(me // 2, NZ)
    y = me // (2 * NZ)
    partner = me + 1 - 2 * core
    rows = glb.shape[0] // n_head
    x = head // 2
    y_lo = lax.rem(head, 2)
    head_rows = pl.ds(mult(head * rows, 16), rows)

    def z_dev(s):
        return {"ctx": (y * NZ + lax.rem(z + s, NZ)) * 2 + core}

    def y_dev(s):
        return {"ctx": (lax.rem(y + s, NY) * NZ + z) * 2 + core}

    def at_head(s):
        return lax.rem(head + s, n_head)

    def remote(src, dst, send, recv, device):
        return pltpu.make_async_remote_copy(
            src_ref=src, dst_ref=dst, send_sem=send, recv_sem=recv, device_id=device, device_id_type=MESH
        )

    def phase(block, send, recv):
        return remote(block, block, send, recv, {"ctx": partner})

    own_block = win.at[:, slot_cols(PREV)]
    loads = [
        pltpu.make_async_copy(src, dst, load_sem.at[i])
        for i, (src, dst) in enumerate(
            [(lat_hbm, own_block), (seg_hbm, seg_ref), (q_hbm, q_ref), (do_hbm, do_ref)]
            + [
                (
                    w.at[:, pl.ds(FIRST[p], WIDE[p])],
                    wcat.at[:, pl.ds(2 * FIRST[p] + kind * WIDE[p], WIDE[p])],
                )
                for p in range(len(PIECES))
                for kind, w in enumerate((wk_hbm, wv_hbm))
            ]
        )
    ]
    for load in loads:
        load.start()

    barrier = pltpu.get_barrier_semaphore()

    def greet(device):
        pl.semaphore_signal(barrier, inc=1, device_id=device, device_id_type=MESH)

    for s in (4, 2, 1, 3):

        @pl.when(me >= s)
        def _():
            greet({"ctx": me - s})

    for s in range(1, n_head):
        greet({"head": at_head(s)})
    greet({"ctx": partner})
    for s in range(1, n_head // 2):
        greet({"ctx": partner, "head": lax.rem(x + s, n_head // 2) * 2 + y_lo})
    for s in range(1, PREV + 1):

        @pl.when(me + s < n_ctx)
        def _():
            greet({"ctx": me + s})

    for s in range(1, NZ):
        greet(z_dev(s))
    for s in range(1, NY):
        greet(y_dev(s))

    pl.semaphore_wait(
        barrier,
        NZ - 1 + NY - 1 + n_head + n_head // 2 - 1 + jnp.minimum(me, PREV) + jnp.minimum(n_ctx - 1 - me, PREV),
    )

    x_peers = n_head // 2
    x_size = (LAT + ROPE) // x_peers
    x_rows = pl.ds(mult(x * x_size, 16), x_size)

    def x_dev(s):
        return {"head": lax.rem(x + s, x_peers) * 2 + y_lo}

    near = remote(lat_hbm, win.at[:, slot_cols(2)], halo_s.at[0], halo_r.at[0], {"ctx": me + 2})
    far = remote(
        lat_hbm.at[x_rows], win.at[x_rows, slot_cols(0)], halo_s.at[1], halo_r.at[1], {"ctx": me + 4}
    )

    def far_copy(s):
        block = win.at[x_rows, slot_cols(0)]
        return remote(block, block, far_s, far_r, x_dev(s))

    def cross_copy(s):
        return remote(
            win.at[x_rows, slot_cols(0)],
            win.at[x_rows, slot_cols(1)],
            mate_s.at[1],
            mate_r.at[1],
            {"ctx": partner} | x_dev(s),
        )

    def mate_copy(i, src):
        return remote(
            lat_hbm if src == PREV else win.at[:, slot_cols(src)],
            win.at[:, slot_cols(PREV - 1 - 2 * i)],
            mate_s.at[i],
            mate_r.at[i],
            {"ctx": partner},
        )

    @pl.when(me + 4 < n_ctx)
    def _():
        far.start()

    @pl.when(me + 2 < n_ctx)
    def _():
        near.start()

    @pl.when(core == 0)
    def _():
        mate_copy(0, PREV).start()

    far_all = phase(win.at[pl.ds(0, (x_peers - 1) * x_size), slot_cols(0)], far_s, far_r)

    for load in loads:
        load.wait()
    for h in range(HEADS):
        block = q_ref[:, pl.ds(h * QK, QK)]
        qs[h] = block
        qt[h] = block.T
        dot[h] = do_ref[:, pl.ds(h * VDIM, VDIM)].T
    own = seg_ref[pl.ds(me, 1), :]
    query_seg = jnp.broadcast_to(own, (TOK, TOK)).T
    for s in range(PREV + 1):
        place = me - PREV + s
        key_seg = jnp.where(place >= 0, seg_ref[pl.ds(jnp.maximum(place, 0), 1), :], -1)
        allowed = query_seg == key_seg
        if s == PREV:
            allowed &= lax.broadcasted_iota(jnp.int32, (TOK, TOK), 1) <= lax.broadcasted_iota(
                jnp.int32, (TOK, TOK), 0
            )
        bias[:, slot_cols(s)] = jnp.where(allowed, 0.0, -jnp.inf)

    @pl.when(me >= 4)
    def _():
        far.wait_recv()
        for s in FAR_Y:
            far_copy(s).start()

        @pl.when(core == 1)
        def _():
            for s in (*FAR_Y, 0):
                cross_copy(s).start()

    for i in range(4):
        wt[pl.ds(i * 256, 256), :] = wcat[:, pl.ds(i * 256, 256)].T
    def project(start, size):
        cols = pl.ds(start, size)
        for p, (heads, _) in enumerate(PIECES):
            first, wide = FIRST[p], WIDE[p]
            made = nn(wt[pl.ds(2 * first, 2 * wide), :], win[pl.ds(0, LAT), cols]).astype(BF)
            for j, h in enumerate(heads):
                kt[h, pl.ds(0, NOPE), cols] = made[j * NOPE : (j + 1) * NOPE]
                vt[h, :, cols] = made[wide + j * VDIM : wide + (j + 1) * VDIM]
        for h in range(HEADS):
            kt[h, pl.ds(NOPE, ROPE), cols] = win[pl.ds(LAT, ROPE), cols]

    def products(start, size):
        cols = pl.ds(start, size)
        for h in range(HEADS):
            raw_scores[h, :, cols] = nn(qs[h], kt[h, :, cols]) * SCALE + bias[:, cols]
            raw_grads[h, :, cols] = nn(do_ref[:, pl.ds(h * VDIM, VDIM)], vt[h, :, cols])

    project(PREV * TOK, TOK)

    @pl.when(me >= 2)
    def _():
        near.wait_recv()

    @pl.when(me < 2)
    def _():
        win[:, slot_cols(2)] = jnp.zeros((LAT + ROPE, TOK), BF)

    @pl.when(core == 0)
    def _():
        mate_copy(1, 2).start()

    @pl.when(core == 1)
    def _():
        mate_copy(0, 2).start()

    mate_copy(0, PREV).wait_recv()
    project(2 * TOK, 2 * TOK)
    products(2 * TOK, 3 * TOK)

    @pl.when(me >= 4)
    def _():
        far_all.wait_recv()

    @pl.when(me < 4)
    def _():
        win[:, slot_cols(0)] = jnp.zeros((LAT + ROPE, TOK), BF)

    @pl.when(me + 4 < n_ctx)
    def _():
        far.wait_send()

    @pl.when(me + 2 < n_ctx)
    def _():
        near.wait_send()

    @pl.when((core == 1) | (me >= 4))
    def _():
        mate_copy(1, PREV).wait_recv()

    @pl.when((core == 0) & (me < 4))
    def _():
        win[:, slot_cols(1)] = jnp.zeros((LAT + ROPE, TOK), BF)

    project(0, 2 * TOK)
    products(0, 2 * TOK)

    mate_copy(0, PREV).wait_send()

    @pl.when((core == 0) | (me >= 4))
    def _():
        mate_copy(1, PREV).wait_send()

    @pl.when(me >= 4)
    def _():
        far_all.wait_send()

    def some_heads(*heads):
        scores = [raw_scores[h] for h in heads]
        expo = [jnp.exp(a - jnp.max(a, axis=1, keepdims=True)) for a in scores]
        scaling = [1.0 / jnp.sum(a, axis=1, keepdims=True) for a in expo]
        out = [(nt(a.astype(BF), vt[h]) * b).astype(BF) for h, a, b in zip(heads, expo, scaling)]
        probs = [a * b for a, b in zip(expo, scaling)]
        for h, a in zip(heads, out):
            attn_ref[:, pl.ds(h * VDIM, VDIM)] = a
        delta = [
            jnp.sum(f32(do_ref[:, pl.ds(h * VDIM, VDIM)]) * f32(a), axis=1, keepdims=True)
            for h, a in zip(heads, out)
        ]
        grad_scores = [
            (a * (raw_grads[h] - b)).astype(BF) for h, a, b in zip(heads, probs, delta)
        ]
        for h, a, b in zip(heads, probs, grad_scores):
            p = [h in group for group, _ in PIECES].index(True)
            base = 2 * FIRST[p] + PIECES[p][0].index(h) * NOPE
            term = (nn(qt[h], b) * SCALE).astype(BF)
            dcat[pl.ds(base, NOPE), :] = term[:NOPE]
            rope_sum[...] = f32(term[NOPE:]) if h == 0 else rope_sum[...] + f32(term[NOPE:])
            dcat[pl.ds(base + WIDE[p], VDIM), :] = nn(dot[h], a.astype(BF)).astype(BF)
        for h, b in zip(heads, grad_scores):
            gq_ref[:, pl.ds(h * QK, QK)] = (nt(b, kt[h]) * SCALE).astype(BF)

    def pair_copy(p):
        return remote(
            part[p].at[1 - core], pair_in[p], pair_s.at[p], pair_r.at[p], {"ctx": partner}
        )

    def weight_terms(p):
        first, wide = FIRST[p], WIDE[p]
        terms = nt(win[pl.ds(0, LAT), :], dcat[pl.ds(2 * first, 2 * wide), :]).astype(BF)
        part[p][0] = terms[:, :wide]
        part[p][1] = terms[:, wide:]
        pair_copy(p).start()

    def z_rows(p, i):
        size = A_ROWS[p] // NZ
        return pl.ds(mult(i * size, size), size)

    def y_rows(p, i):
        size = B_ROWS[p] // NY
        return pl.ds(mult(A_ROWS[p] + i * size, size), size)

    def piece_cols(p):
        return pl.ds(FIRST[p], WIDE[p])

    def small(p, i):
        return pl.ds(mult(i // 2 * 16, 16), 16), pl.ds(mult(lax.rem(i, 2) * (WIDE[p] // 2), 128), WIDE[p] // 2)

    def z_copy(p, s):
        return remote(
            half[p].at[z_rows(p, lax.rem(z + s, NZ))], z_in[p].at[s - 1], z_s.at[p], z_r.at[p], z_dev(s)
        )

    def y_copy(p, s):
        return remote(
            half[p].at[y_rows(p, lax.rem(y + s, NY))], y_in[p].at[s - 1], y_s.at[p], y_r.at[p], y_dev(s)
        )

    def zy_copy(p, s):
        return remote(zy_all[p].at[y], zy_all[p].at[y], zy_s.at[p], zy_r.at[p], y_dev(s))

    def yz_copy(p, s):
        r, c = small(p, lax.rem(z + s, NZ))
        return remote(y_part[p].at[r, c], yz_in[p].at[s - 1], yz_s.at[p], yz_r.at[p], z_dev(s))

    def z_place(p):
        return gw_ref.at[z_rows(p, z), piece_cols(p)]

    def y_place(p):
        return gw_ref.at[y_rows(p, y), piece_cols(p)]

    def yz_place(p):
        size = B_ROWS[p] // NY
        r = pl.ds(mult(A_ROWS[p] + y * size + z // 2 * 16, 16), 16)
        return gw_ref.at[r, pl.ds(mult(FIRST[p] + lax.rem(z, 2) * (WIDE[p] // 2), 128), WIDE[p] // 2)]

    def yzg_copy(p, s):
        return remote(yz_place(p), yz_place(p), yzg_s.at[p], yzg_r.at[p], z_dev(s))

    def zg_copy(p, s):
        return remote(z_place(p), z_place(p), zg_s.at[p], zg_r.at[p], z_dev(s))

    def yg_copy(p, s):
        return remote(y_place(p), y_place(p), yg_s.at[p], yg_r.at[p], y_dev(s))

    def pairg_copy(p):
        return remote(
            gw_ref.at[:, piece_cols(p)],
            gw_out.at[core, :, piece_cols(p)],
            pairg_s.at[p],
            pairg_r.at[p],
            {"ctx": partner},
        )

    def keep_copy(p):
        return pltpu.make_async_copy(
            gw_ref.at[:, piece_cols(p)], gw_out.at[core, :, piece_cols(p)], store_sem.at[p]
        )

    def z_phase(p):
        return phase(z_in[p], z_s.at[p], z_r.at[p])

    def y_phase(p):
        return phase(y_in[p], y_s.at[p], y_r.at[p])

    def zy_phase(p):
        return phase(zy_all[p].at[pl.ds(0, NY - 1)], zy_s.at[p], zy_r.at[p])

    def yz_phase(p):
        return phase(yz_in[p], yz_s.at[p], yz_r.at[p])

    def yzg_phase(p):
        return phase(yz_in[p], yzg_s.at[p], yzg_r.at[p])

    def zg_phase(p):
        return phase(z_in[p], zg_s.at[p], zg_r.at[p])

    def yg_phase(p):
        return phase(y_in[p], yg_s.at[p], yg_r.at[p])

    def stage_a(p):
        pair_copy(p).wait_recv()
        a, b = pl.ds(0, A_ROWS[p]), pl.ds(A_ROWS[p], B_ROWS[p])
        if B_ROWS[p]:
            half[p][b, :] = (f32(part[p][core, b, :]) + f32(pair_in[p][b, :])).astype(BF)
            for s in FAR_Y:
                y_copy(p, s).start()
        half[p][a, :] = (f32(part[p][core, a, :]) + f32(pair_in[p][a, :])).astype(BF)
        for s in FAR_Z:
            z_copy(p, s).start()
        pair_copy(p).wait_send()

    def stage_b(p):
        if B_ROWS[p]:
            y_phase(p).wait_recv()
            total = f32(half[p][y_rows(p, y), :])
            for s in range(1, NY):
                total += f32(y_in[p][s - 1])
            y_part[p][...] = total.astype(BF)
            for s in FAR_Z:
                yz_copy(p, s).start()
        z_phase(p).wait_recv()
        total = f32(half[p][z_rows(p, z), :])
        for s in range(1, NZ):
            total += f32(z_in[p][s - 1])
        zy_all[p][y] = total.astype(BF)
        for s in FAR_Y:
            zy_copy(p, s).start()
        z_phase(p).wait_send()
        if B_ROWS[p]:
            y_phase(p).wait_send()

    def stage_c(p):
        if B_ROWS[p]:
            yz_phase(p).wait_recv()
            r, c = small(p, z)
            total = f32(y_part[p][r, c])
            for s in range(1, NZ):
                total += f32(yz_in[p][s - 1])
            yz_place(p)[...] = total.astype(BF)
            for s in FAR_Z:
                yzg_copy(p, s).start()
        zy_phase(p).wait_recv()
        total = f32(zy_all[p][0])
        for i in range(1, NY):
            total += f32(zy_all[p][i])
        z_place(p)[...] = total.astype(BF)
        for s in FAR_Z:
            zg_copy(p, s).start()
        zy_phase(p).wait_send()
        if B_ROWS[p]:
            yz_phase(p).wait_send()

    def stage_d(p):
        yzg_phase(p).wait_recv()
        for s in FAR_Y:
            yg_copy(p, s).start()
        yzg_phase(p).wait_send()

    def stage_e(p):
        zg_phase(p).wait_recv()
        if B_ROWS[p]:
            yg_phase(p).wait_recv()
        pairg_copy(p).start()
        keep_copy(p).start()
        zg_phase(p).wait_send()
        if B_ROWS[p]:
            yg_phase(p).wait_send()

    def x_copy(s):
        there = lax.rem(x + s, x_peers)
        return remote(
            glb.at[pl.ds(mult(there * 2 * rows, 16), 2 * rows)],
            x_in.at[s - 1],
            x_s,
            x_r,
            x_dev(s),
        )

    def yl_copy():
        return remote(
            x_part.at[pl.ds(mult((1 - y_lo) * rows, 16), rows)],
            yl_in,
            yl_s,
            yl_r,
            {"head": head + 1 - 2 * y_lo},
        )

    def ctx_copy(s):
        return remote(
            ctx_part.at[:, slot_cols(PREV - s)],
            ctx_in.at[s - 1],
            ctx_s.at[s - 1],
            ctx_r.at[s - 1],
            {"ctx": me - s},
        )

    def headg_copy(s):
        return remote(
            gl_ref.at[head_rows], gl_out.at[head_rows], headg_s, headg_r, {"head": at_head(s)}
        )

    def own_rows():
        return pltpu.make_async_copy(gl_ref.at[head_rows], gl_out.at[head_rows], store_sem.at[len(PIECES)])

    def head_outputs():
        return [
            pltpu.make_async_copy(attn_ref, attn_out, store_sem.at[len(PIECES) + 1]),
            pltpu.make_async_copy(gq_ref, gq_out, store_sem.at[len(PIECES) + 2]),
        ]

    def latent_terms():
        glb[pl.ds(0, LAT), :] = nn(wcat[...], dcat[...]).astype(BF)
        glb[pl.ds(LAT, ROPE), :] = rope_sum[...].astype(BF)
        glb[pl.ds(LAT + ROPE, glb.shape[0] - LAT - ROPE), :] = jnp.zeros(
            (glb.shape[0] - LAT - ROPE, WIN), BF
        )
        for s in FAR_Y:
            x_copy(s).start()

    def latent_x():
        phase(x_in, x_s, x_r).wait_recv()
        total = f32(glb[pl.ds(mult(x * 2 * rows, 16), 2 * rows), :])
        for s in range(1, x_peers):
            total += f32(x_in[s - 1])
        x_part[...] = total.astype(BF)
        yl_copy().start()
        phase(x_in, x_s, x_r).wait_send()

    def latent_y():
        yl_copy().wait_recv()
        total = f32(x_part[pl.ds(mult(y_lo * rows, 16), rows), :]) + f32(yl_in[...])
        ctx_part[...] = total.astype(BF)
        for s in range(1, PREV + 1):

            @pl.when(me >= s)
            def _():
                ctx_copy(s).start()

        yl_copy().wait_send()

    def latent_blocks():
        for s in range(1, PREV + 1):

            @pl.when(me + s < n_ctx)
            def _():
                ctx_copy(s).wait_recv()

            @pl.when(me + s >= n_ctx)
            def _():
                ctx_in[s - 1] = jnp.zeros(ctx_in.shape[1:], BF)

        total = f32(ctx_part[:, slot_cols(PREV)])
        for s in range(1, PREV + 1):
            total += f32(ctx_in[s - 1])
        gl_ref[head_rows, :] = total.astype(BF)
        for s in FAR_Z:
            headg_copy(s).start()
        own_rows().start()

    some_heads(0, 1)
    weight_terms(0)
    some_heads(2, 3)
    stage_a(0)
    weight_terms(1)
    latent_terms()
    for copy in head_outputs():
        copy.start()
    stage_a(1)
    stage_b(0)
    stage_b(1)
    stage_c(0)
    stage_c(1)
    latent_x()
    stage_d(0)
    stage_d(1)
    latent_y()
    stage_e(0)
    latent_blocks()
    stage_e(1)

    for s in range(1, PREV + 1):

        @pl.when(me >= s)
        def _():
            ctx_copy(s).wait_send()

    phase(gl_out.at[pl.ds(0, (n_head - 1) * rows)], headg_s, headg_r).wait()
    own_rows().wait()
    for copy in head_outputs():
        copy.wait()
    for p in range(len(PIECES)):
        pairg_copy(p).wait()
        keep_copy(p).wait()


def write_out(attn, gq, gl, gw, attn_out, gq_out, gl_out, gk_out, gv_out, *rest):
    stages, load_sem, store_sem = rest[:5], rest[5], rest[6]
    parts = [(gw.at[k, pl.ds(i * 128, 128)], out.at[pl.ds(i * 128, 128)]) for k, out in ((0, gk_out), (1, gv_out)) for i in range(4)]
    parts += [(gq, gq_out), (gl.at[pl.ds(0, LAT + ROPE)], gl_out), (attn, attn_out)]
    spots = [stages[0].at[pl.ds(i * 128, 128)] for i in range(4)]
    spots += [stages[1].at[pl.ds(i * 128, 128)] for i in range(4)]
    spots += list(stages[2:])
    loads = [
        pltpu.make_async_copy(src, spot, load_sem.at[i])
        for i, ((src, _), spot) in enumerate(zip(parts, spots))
    ]
    stores = [
        pltpu.make_async_copy(spot, dst, store_sem.at[i])
        for i, ((_, dst), spot) in enumerate(zip(parts, spots))
    ]
    for load in loads:
        load.start()
    for load, store in zip(loads, stores):
        load.wait()
        store.start()
    for store in stores:
        store.wait()


def per_device(queries, latent, w_key, w_value, grad_out, segment_ids):
    n_ctx = lax.axis_size("ctx")
    n_head = lax.axis_size("head")
    hbm = pl.BlockSpec(memory_space=pltpu.HBM)
    dma = pltpu.SemaphoreType.DMA
    rows = 80

    def buf(*shape, dtype=BF):
        return pltpu.VMEM(shape, dtype)

    def sems(*shape):
        return [dma(shape), dma(shape)]

    attn_out, grad_queries, grad_latent, grad_w = pl.pallas_call(
        functools.partial(kernel, n_ctx, n_head),
        out_shape=[
            jax.ShapeDtypeStruct((TOK, HEADS * VDIM), BF),
            jax.ShapeDtypeStruct((TOK, HEADS * QK), BF),
            jax.ShapeDtypeStruct((rows * n_head, TOK), BF),
            jax.ShapeDtypeStruct((2, LAT, HEADS * NOPE), BF),
        ],
        in_specs=[hbm] * 6,
        out_specs=[hbm] * 4,
        scratch_shapes=[
            buf(TOK, HEADS * VDIM),
            buf(TOK, HEADS * QK),
            buf(rows * n_head, TOK),
            buf(LAT, HEADS * NOPE),
            buf(TOK, HEADS * QK),
            buf(LAT, 2 * HEADS * NOPE),
            buf(TOK, HEADS * VDIM),
            buf(n_ctx, TOK, dtype=jnp.int32),
            buf(LAT + ROPE, WIN),
            buf(2 * HEADS * NOPE, LAT),
            buf(HEADS, TOK, QK),
            buf(HEADS, QK, TOK),
            buf(HEADS, VDIM, TOK),
            buf(HEADS, QK, WIN),
            buf(HEADS, VDIM, WIN),
            buf(TOK, WIN, dtype=jnp.float32),
            buf(HEADS, TOK, WIN, dtype=jnp.float32),
            buf(HEADS, TOK, WIN, dtype=jnp.float32),
            buf(2 * HEADS * NOPE, WIN),
            buf(ROPE, WIN, dtype=jnp.float32),
            *[buf(2, LAT, wide) for wide in WIDE],
            *[buf(LAT, wide) for wide in WIDE],
            *[buf(LAT, wide) for wide in WIDE],
            *[buf(NZ - 1, a // NZ, wide) for a, wide in zip(A_ROWS, WIDE)],
            *[buf(NY, a // NZ, wide) for a, wide in zip(A_ROWS, WIDE)],
            *[buf(NY - 1, max(b // NY, 16), wide) for b, wide in zip(B_ROWS, WIDE)],
            *[buf(NZ - 1, 16, max(wide // 2, 128)) for wide in WIDE],
            *[buf(max(b // NY, 16), wide) for b, wide in zip(B_ROWS, WIDE)],
            buf(rows * n_head, WIN),
            buf(n_head // 2 - 1, 2 * rows, WIN),
            buf(2 * rows, WIN),
            buf(rows, WIN),
            buf(rows, WIN),
            buf(PREV, rows, TOK),
            dma((4 + 2 * len(PIECES),)),
            *sems(2),
            dma,
            dma,
            *sems(2),
            *sems(len(PIECES)),
            *sems(len(PIECES)),
            *sems(len(PIECES)),
            *sems(len(PIECES)),
            *sems(len(PIECES)),
            *sems(len(PIECES)),
            *sems(len(PIECES)),
            *sems(len(PIECES)),
            *sems(len(PIECES)),
            dma,
            dma,
            dma,
            dma,
            *sems(PREV),
            dma,
            dma,
            dma((len(PIECES) + 3,)),
        ],
        compiler_params=pltpu.CompilerParams(
            collective_id=0, has_side_effects=True, vmem_limit_bytes=60 * 2**20
        ),
        name="attention",
    )(queries, latent.T, w_key, w_value, grad_out, segment_ids.reshape(n_ctx, TOK))
    any_space = pl.BlockSpec(memory_space=pl.ANY)
    attn_out, grad_queries, grad_latent, grad_w_key, grad_w_value = pl.pallas_call(
        write_out,
        out_shape=[
            jax.ShapeDtypeStruct((TOK, HEADS * VDIM), BF),
            jax.ShapeDtypeStruct((TOK, HEADS * QK), BF),
            jax.ShapeDtypeStruct((LAT + ROPE, TOK), BF),
            jax.ShapeDtypeStruct((LAT, HEADS * NOPE), BF),
            jax.ShapeDtypeStruct((LAT, HEADS * NOPE), BF),
        ],
        in_specs=[any_space] * 4,
        out_specs=[hbm] * 5,
        scratch_shapes=[
            buf(LAT, HEADS * NOPE),
            buf(LAT, HEADS * NOPE),
            buf(TOK, HEADS * QK),
            buf(LAT + ROPE, TOK),
            buf(TOK, HEADS * VDIM),
            *sems(11),
        ],
        compiler_params=pltpu.CompilerParams(vmem_limit_bytes=60 * 2**20),
        name="write_out",
    )(attn_out, grad_queries, grad_latent, grad_w)
    return (attn_out, grad_queries, grad_latent.T, grad_w_key, grad_w_value)


def solution(mesh):
    return jax.shard_map(
        per_device,
        mesh=mesh,
        in_specs=(
            P("ctx", "head"),
            P("ctx", None),
            P(None, "head"),
            P(None, "head"),
            P("ctx", "head"),
            P(),
        ),
        out_specs=(
            P("ctx", "head"),
            P("ctx", "head"),
            P("ctx", None),
            P(None, "head"),
            P(None, "head"),
        ),
        check_vma=False,
    )
```

```python
import functools
import math

import jax
import jax.numpy as jnp
from jax import lax
from jax.experimental import pallas as pl
from jax.experimental.pallas import tpu as pltpu
from jax.sharding import PartitionSpec as P

LAT = 512
ROPE = 64
NOPE = 128
VDIM = 128
PREV = 4
NZ = 8
NY = 4
TOK = 128
WIN = (PREV + 1) * TOK
QK = NOPE + ROPE
HEADS = 4
PIECES = (((0, 1), 256), ((2, 3), 256))
WIDE = [len(heads) * NOPE for heads, _ in PIECES]
FIRST = [heads[0] * NOPE for heads, _ in PIECES]
A_ROWS = [a_rows for _, a_rows in PIECES]
B_ROWS = [512 - a_rows for a_rows in A_ROWS]
FAR_Z = (4, 3, 5, 2, 6, 1, 7)
FAR_Y = (2, 1, 3)
MESH = pl.DeviceIdType.MESH
BF = jnp.bfloat16
SCALE = 1.0 / math.sqrt(QK)


def f32(x):
    return x.astype(jnp.float32)


def nn(a, b):
    return jnp.dot(a, b, preferred_element_type=jnp.float32)


def nt(a, b):
    return lax.dot_general(a, b, (((1,), (1,)), ((), ())), preferred_element_type=jnp.float32)


def mult(x, m):
    return pl.multiple_of(x, m)


def slot_cols(slot):
    return pl.ds(slot * TOK, TOK)


def kernel(n_ctx, n_head, *refs):
    (
        q_hbm,
        lat_hbm,
        wk_hbm,
        wv_hbm,
        do_hbm,
        seg_hbm,
        attn_out,
        gq_out,
        gl_out,
        gw_out,
        attn_ref,
        gq_ref,
        gl_ref,
        gw_ref,
        q_ref,
        wcat,
        do_ref,
        seg_ref,
        win,
        wt,
        qs,
        qt,
        dot,
        kt,
        vt,
        bias,
        raw_scores,
        raw_grads,
        dcat,
        rope_sum,
        *by_piece,
        glb,
        x_in,
        x_part,
        yl_in,
        ctx_part,
        ctx_in,
        load_sem,
        halo_s,
        halo_r,
        far_s,
        far_r,
        mate_s,
        mate_r,
        pair_s,
        pair_r,
        z_s,
        z_r,
        y_s,
        y_r,
        zy_s,
        zy_r,
        yz_s,
        yz_r,
        yzg_s,
        yzg_r,
        zg_s,
        zg_r,
        yg_s,
        yg_r,
        pairg_s,
        pairg_r,
        x_s,
        x_r,
        yl_s,
        yl_r,
        ctx_s,
        ctx_r,
        headg_s,
        headg_r,
        store_sem,
    ) = refs
    part, pair_in, half, z_in, zy_all, y_in, yz_in, y_part = (
        by_piece[i * len(PIECES) : (i + 1) * len(PIECES)] for i in range(8)
    )
    me = lax.axis_index("ctx")
    head = lax.axis_index("head")
    core = lax.rem(me, 2)
    z = lax.rem(me // 2, NZ)
    y = me // (2 * NZ)
    partner = me + 1 - 2 * core
    rows = glb.shape[0] // n_head
    x = head // 2
    y_lo = lax.rem(head, 2)
    head_rows = pl.ds(mult(head * rows, 16), rows)

    def z_dev(s):
        return {"ctx": (y * NZ + lax.rem(z + s, NZ)) * 2 + core}

    def y_dev(s):
        return {"ctx": (lax.rem(y + s, NY) * NZ + z) * 2 + core}

    def at_head(s):
        return lax.rem(head + s, n_head)

    def remote(src, dst, send, recv, device):
        return pltpu.make_async_remote_copy(
            src_ref=src, dst_ref=dst, send_sem=send, recv_sem=recv, device_id=device, device_id_type=MESH
        )

    def phase(block, send, recv):
        return remote(block, block, send, recv, {"ctx": partner})

    own_block = win.at[:, slot_cols(PREV)]
    loads = [
        pltpu.make_async_copy(src, dst, load_sem.at[i])
        for i, (src, dst) in enumerate(
            [(lat_hbm, own_block), (seg_hbm, seg_ref), (q_hbm, q_ref), (do_hbm, do_ref)]
            + [
                (
                    w.at[:, pl.ds(FIRST[p], WIDE[p])],
                    wcat.at[:, pl.ds(2 * FIRST[p] + kind * WIDE[p], WIDE[p])],
                )
                for p in range(len(PIECES))
                for kind, w in enumerate((wk_hbm, wv_hbm))
            ]
        )
    ]
    for load in loads:
        load.start()

    barrier = pltpu.get_barrier_semaphore()

    def greet(device):
        pl.semaphore_signal(barrier, inc=1, device_id=device, device_id_type=MESH)

    for s in (4, 2, 1, 3):

        @pl.when(me >= s)
        def _():
            greet({"ctx": me - s})

    for s in range(1, n_head):
        greet({"head": at_head(s)})
    greet({"ctx": partner})
    for s in range(1, n_head // 2):
        greet({"ctx": partner, "head": lax.rem(x + s, n_head // 2) * 2 + y_lo})
    for s in range(1, PREV + 1):

        @pl.when(me + s < n_ctx)
        def _():
            greet({"ctx": me + s})

    for s in range(1, NZ):
        greet(z_dev(s))
    for s in range(1, NY):
        greet(y_dev(s))

    pl.semaphore_wait(
        barrier,
        NZ - 1 + NY - 1 + n_head + n_head // 2 - 1 + jnp.minimum(me, PREV) + jnp.minimum(n_ctx - 1 - me, PREV),
    )

    x_peers = n_head // 2
    x_size = (LAT + ROPE) // x_peers
    x_rows = pl.ds(mult(x * x_size, 16), x_size)

    def x_dev(s):
        return {"head": lax.rem(x + s, x_peers) * 2 + y_lo}

    near = remote(lat_hbm, win.at[:, slot_cols(2)], halo_s.at[0], halo_r.at[0], {"ctx": me + 2})
    far = remote(
        lat_hbm.at[x_rows], win.at[x_rows, slot_cols(0)], halo_s.at[1], halo_r.at[1], {"ctx": me + 4}
    )

    def far_copy(s):
        block = win.at[x_rows, slot_cols(0)]
        return remote(block, block, far_s, far_r, x_dev(s))

    def cross_copy(s):
        return remote(
            win.at[x_rows, slot_cols(0)],
            win.at[x_rows, slot_cols(1)],
            mate_s.at[1],
            mate_r.at[1],
            {"ctx": partner} | x_dev(s),
        )

    def mate_copy(i, src):
        return remote(
            lat_hbm if src == PREV else win.at[:, slot_cols(src)],
            win.at[:, slot_cols(PREV - 1 - 2 * i)],
            mate_s.at[i],
            mate_r.at[i],
            {"ctx": partner},
        )

    @pl.when(me + 4 < n_ctx)
    def _():
        far.start()

    @pl.when(me + 2 < n_ctx)
    def _():
        near.start()

    @pl.when(core == 0)
    def _():
        mate_copy(0, PREV).start()

    far_all = phase(win.at[pl.ds(0, (x_peers - 1) * x_size), slot_cols(0)], far_s, far_r)

    for load in loads:
        load.wait()
    for h in range(HEADS):
        block = q_ref[:, pl.ds(h * QK, QK)]
        qs[h] = block
        qt[h] = block.T
        dot[h] = do_ref[:, pl.ds(h * VDIM, VDIM)].T
    own = seg_ref[pl.ds(me, 1), :]
    query_seg = jnp.broadcast_to(own, (TOK, TOK)).T
    for s in range(PREV + 1):
        place = me - PREV + s
        key_seg = jnp.where(place >= 0, seg_ref[pl.ds(jnp.maximum(place, 0), 1), :], -1)
        allowed = query_seg == key_seg
        if s == PREV:
            allowed &= lax.broadcasted_iota(jnp.int32, (TOK, TOK), 1) <= lax.broadcasted_iota(
                jnp.int32, (TOK, TOK), 0
            )
        bias[:, slot_cols(s)] = jnp.where(allowed, 0.0, -jnp.inf)

    @pl.when(me >= 4)
    def _():
        far.wait_recv()
        for s in FAR_Y:
            far_copy(s).start()

        @pl.when(core == 1)
        def _():
            for s in (*FAR_Y, 0):
                cross_copy(s).start()

    for i in range(4):
        wt[pl.ds(i * 256, 256), :] = wcat[:, pl.ds(i * 256, 256)].T
    def project(start, size):
        cols = pl.ds(start, size)
        for p, (heads, _) in enumerate(PIECES):
            first, wide = FIRST[p], WIDE[p]
            made = nn(wt[pl.ds(2 * first, 2 * wide), :], win[pl.ds(0, LAT), cols]).astype(BF)
            for j, h in enumerate(heads):
                kt[h, pl.ds(0, NOPE), cols] = made[j * NOPE : (j + 1) * NOPE]
                vt[h, :, cols] = made[wide + j * VDIM : wide + (j + 1) * VDIM]
        for h in range(HEADS):
            kt[h, pl.ds(NOPE, ROPE), cols] = win[pl.ds(LAT, ROPE), cols]

    def products(start, size):
        cols = pl.ds(start, size)
        for h in range(HEADS):
            raw_scores[h, :, cols] = nn(qs[h], kt[h, :, cols]) * SCALE + bias[:, cols]
            raw_grads[h, :, cols] = nn(do_ref[:, pl.ds(h * VDIM, VDIM)], vt[h, :, cols])

    project(PREV * TOK, TOK)

    @pl.when(me >= 2)
    def _():
        near.wait_recv()

    @pl.when(me < 2)
    def _():
        win[:, slot_cols(2)] = jnp.zeros((LAT + ROPE, TOK), BF)

    @pl.when(core == 0)
    def _():
        mate_copy(1, 2).start()

    @pl.when(core == 1)
    def _():
        mate_copy(0, 2).start()

    mate_copy(0, PREV).wait_recv()
    project(2 * TOK, 2 * TOK)
    products(2 * TOK, 3 * TOK)

    @pl.when(me >= 4)
    def _():
        far_all.wait_recv()

    @pl.when(me < 4)
    def _():
        win[:, slot_cols(0)] = jnp.zeros((LAT + ROPE, TOK), BF)

    @pl.when(me + 4 < n_ctx)
    def _():
        far.wait_send()

    @pl.when(me + 2 < n_ctx)
    def _():
        near.wait_send()

    @pl.when((core == 1) | (me >= 4))
    def _():
        mate_copy(1, PREV).wait_recv()

    @pl.when((core == 0) & (me < 4))
    def _():
        win[:, slot_cols(1)] = jnp.zeros((LAT + ROPE, TOK), BF)

    project(0, 2 * TOK)
    products(0, 2 * TOK)

    mate_copy(0, PREV).wait_send()

    @pl.when((core == 0) | (me >= 4))
    def _():
        mate_copy(1, PREV).wait_send()

    @pl.when(me >= 4)
    def _():
        far_all.wait_send()

    def some_heads(*heads):
        scores = [raw_scores[h] for h in heads]
        expo = [jnp.exp(a - jnp.max(a, axis=1, keepdims=True)) for a in scores]
        scaling = [1.0 / jnp.sum(a, axis=1, keepdims=True) for a in expo]
        out = [(nt(a.astype(BF), vt[h]) * b).astype(BF) for h, a, b in zip(heads, expo, scaling)]
        probs = [a * b for a, b in zip(expo, scaling)]
        for h, a in zip(heads, out):
            attn_ref[:, pl.ds(h * VDIM, VDIM)] = a
        delta = [
            jnp.sum(f32(do_ref[:, pl.ds(h * VDIM, VDIM)]) * f32(a), axis=1, keepdims=True)
            for h, a in zip(heads, out)
        ]
        grad_scores = [
            (a * (raw_grads[h] - b)).astype(BF) for h, a, b in zip(heads, probs, delta)
        ]
        for h, a, b in zip(heads, probs, grad_scores):
            p = [h in group for group, _ in PIECES].index(True)
            base = 2 * FIRST[p] + PIECES[p][0].index(h) * NOPE
            term = (nn(qt[h], b) * SCALE).astype(BF)
            dcat[pl.ds(base, NOPE), :] = term[:NOPE]
            rope_sum[...] = f32(term[NOPE:]) if h == 0 else rope_sum[...] + f32(term[NOPE:])
            dcat[pl.ds(base + WIDE[p], VDIM), :] = nn(dot[h], a.astype(BF)).astype(BF)
        for h, b in zip(heads, grad_scores):
            gq_ref[:, pl.ds(h * QK, QK)] = (nt(b, kt[h]) * SCALE).astype(BF)

    def pair_copy(p):
        return remote(
            part[p].at[1 - core], pair_in[p], pair_s.at[p], pair_r.at[p], {"ctx": partner}
        )

    def weight_terms(p):
        first, wide = FIRST[p], WIDE[p]
        terms = nt(win[pl.ds(0, LAT), :], dcat[pl.ds(2 * first, 2 * wide), :]).astype(BF)
        part[p][0] = terms[:, :wide]
        part[p][1] = terms[:, wide:]
        pair_copy(p).start()

    def z_rows(p, i):
        size = A_ROWS[p] // NZ
        return pl.ds(mult(i * size, size), size)

    def y_rows(p, i):
        size = B_ROWS[p] // NY
        return pl.ds(mult(A_ROWS[p] + i * size, size), size)

    def piece_cols(p):
        return pl.ds(FIRST[p], WIDE[p])

    def small(p, i):
        return pl.ds(mult(i // 2 * 16, 16), 16), pl.ds(mult(lax.rem(i, 2) * (WIDE[p] // 2), 128), WIDE[p] // 2)

    def z_copy(p, s):
        return remote(
            half[p].at[z_rows(p, lax.rem(z + s, NZ))], z_in[p].at[s - 1], z_s.at[p], z_r.at[p], z_dev(s)
        )

    def y_copy(p, s):
        return remote(
            half[p].at[y_rows(p, lax.rem(y + s, NY))], y_in[p].at[s - 1], y_s.at[p], y_r.at[p], y_dev(s)
        )

    def zy_copy(p, s):
        return remote(zy_all[p].at[y], zy_all[p].at[y], zy_s.at[p], zy_r.at[p], y_dev(s))

    def yz_copy(p, s):
        r, c = small(p, lax.rem(z + s, NZ))
        return remote(y_part[p].at[r, c], yz_in[p].at[s - 1], yz_s.at[p], yz_r.at[p], z_dev(s))

    def z_place(p):
        return gw_ref.at[z_rows(p, z), piece_cols(p)]

    def y_place(p):
        return gw_ref.at[y_rows(p, y), piece_cols(p)]

    def yz_place(p):
        size = B_ROWS[p] // NY
        r = pl.ds(mult(A_ROWS[p] + y * size + z // 2 * 16, 16), 16)
        return gw_ref.at[r, pl.ds(mult(FIRST[p] + lax.rem(z, 2) * (WIDE[p] // 2), 128), WIDE[p] // 2)]

    def yzg_copy(p, s):
        return remote(yz_place(p), yz_place(p), yzg_s.at[p], yzg_r.at[p], z_dev(s))

    def zg_copy(p, s):
        return remote(z_place(p), z_place(p), zg_s.at[p], zg_r.at[p], z_dev(s))

    def yg_copy(p, s):
        return remote(y_place(p), y_place(p), yg_s.at[p], yg_r.at[p], y_dev(s))

    def pairg_copy(p):
        return remote(
            gw_ref.at[:, piece_cols(p)],
            gw_out.at[core, :, piece_cols(p)],
            pairg_s.at[p],
            pairg_r.at[p],
            {"ctx": partner},
        )

    def keep_copy(p):
        return pltpu.make_async_copy(
            gw_ref.at[:, piece_cols(p)], gw_out.at[core, :, piece_cols(p)], store_sem.at[p]
        )

    def z_phase(p):
        return phase(z_in[p], z_s.at[p], z_r.at[p])

    def y_phase(p):
        return phase(y_in[p], y_s.at[p], y_r.at[p])

    def zy_phase(p):
        return phase(zy_all[p].at[pl.ds(0, NY - 1)], zy_s.at[p], zy_r.at[p])

    def yz_phase(p):
        return phase(yz_in[p], yz_s.at[p], yz_r.at[p])

    def yzg_phase(p):
        return phase(yz_in[p], yzg_s.at[p], yzg_r.at[p])

    def zg_phase(p):
        return phase(z_in[p], zg_s.at[p], zg_r.at[p])

    def yg_phase(p):
        return phase(y_in[p], yg_s.at[p], yg_r.at[p])

    def stage_a(p):
        pair_copy(p).wait_recv()
        a, b = pl.ds(0, A_ROWS[p]), pl.ds(A_ROWS[p], B_ROWS[p])
        if B_ROWS[p]:
            half[p][b, :] = (f32(part[p][core, b, :]) + f32(pair_in[p][b, :])).astype(BF)
            for s in FAR_Y:
                y_copy(p, s).start()
        half[p][a, :] = (f32(part[p][core, a, :]) + f32(pair_in[p][a, :])).astype(BF)
        for s in FAR_Z:
            z_copy(p, s).start()
        pair_copy(p).wait_send()

    def stage_b(p):
        if B_ROWS[p]:
            y_phase(p).wait_recv()
            total = f32(half[p][y_rows(p, y), :])
            for s in range(1, NY):
                total += f32(y_in[p][s - 1])
            y_part[p][...] = total.astype(BF)
            for s in FAR_Z:
                yz_copy(p, s).start()
        z_phase(p).wait_recv()
        total = f32(half[p][z_rows(p, z), :])
        for s in range(1, NZ):
            total += f32(z_in[p][s - 1])
        zy_all[p][y] = total.astype(BF)
        for s in FAR_Y:
            zy_copy(p, s).start()
        z_phase(p).wait_send()
        if B_ROWS[p]:
            y_phase(p).wait_send()

    def stage_c(p):
        if B_ROWS[p]:
            yz_phase(p).wait_recv()
            r, c = small(p, z)
            total = f32(y_part[p][r, c])
            for s in range(1, NZ):
                total += f32(yz_in[p][s - 1])
            yz_place(p)[...] = total.astype(BF)
            for s in FAR_Z:
                yzg_copy(p, s).start()
        zy_phase(p).wait_recv()
        total = f32(zy_all[p][0])
        for i in range(1, NY):
            total += f32(zy_all[p][i])
        z_place(p)[...] = total.astype(BF)
        for s in FAR_Z:
            zg_copy(p, s).start()
        zy_phase(p).wait_send()
        if B_ROWS[p]:
            yz_phase(p).wait_send()

    def stage_d(p):
        yzg_phase(p).wait_recv()
        for s in FAR_Y:
            yg_copy(p, s).start()
        yzg_phase(p).wait_send()

    def stage_e(p):
        zg_phase(p).wait_recv()
        if B_ROWS[p]:
            yg_phase(p).wait_recv()
        pairg_copy(p).start()
        keep_copy(p).start()
        zg_phase(p).wait_send()
        if B_ROWS[p]:
            yg_phase(p).wait_send()

    x_full = 2 * rows
    x_last = LAT + ROPE - (x_peers - 1) * x_full

    def x_copy(s, size):
        there = lax.rem(x + s, x_peers)
        return remote(
            glb.at[pl.ds(mult(there * x_full, 16), size)],
            x_in.at[s - 1, pl.ds(0, size)],
            x_s,
            x_r,
            x_dev(s),
        )

    def yl_copy():
        return remote(
            x_part.at[pl.ds(mult((1 - y_lo) * rows, 16), rows)],
            yl_in,
            yl_s,
            yl_r,
            {"head": head + 1 - 2 * y_lo},
        )

    def ctx_copy(s):
        return remote(
            ctx_part.at[:, slot_cols(PREV - s)],
            ctx_in.at[s - 1],
            ctx_s.at[s - 1],
            ctx_r.at[s - 1],
            {"ctx": me - s},
        )

    def headg_copy(s):
        return remote(
            gl_ref.at[head_rows], gl_out.at[head_rows], headg_s, headg_r, {"head": at_head(s)}
        )

    def own_rows():
        return pltpu.make_async_copy(gl_ref.at[head_rows], gl_out.at[head_rows], store_sem.at[len(PIECES)])

    def head_outputs():
        return [
            pltpu.make_async_copy(attn_ref, attn_out, store_sem.at[len(PIECES) + 1]),
            pltpu.make_async_copy(gq_ref, gq_out, store_sem.at[len(PIECES) + 2]),
        ]

    def latent_terms():
        glb[pl.ds(0, LAT), :] = nn(wcat[...], dcat[...]).astype(BF)
        glb[pl.ds(LAT, ROPE), :] = rope_sum[...].astype(BF)
        glb[pl.ds(LAT + ROPE, glb.shape[0] - LAT - ROPE), :] = jnp.zeros(
            (glb.shape[0] - LAT - ROPE, WIN), BF
        )
        for s in FAR_Y:

            @pl.when(lax.rem(x + s, x_peers) < x_peers - 1)
            def _():
                x_copy(s, x_full).start()

            @pl.when(lax.rem(x + s, x_peers) == x_peers - 1)
            def _():
                x_copy(s, x_last).start()


    def latent_x():
        @pl.when(x < x_peers - 1)
        def _():
            phase(x_in, x_s, x_r).wait_recv()

        @pl.when(x == x_peers - 1)
        def _():
            x_in[:, pl.ds(x_last, x_full - x_last), :] = jnp.zeros(
                (x_peers - 1, x_full - x_last, WIN), BF
            )
            phase(x_in.at[:, pl.ds(0, x_last)], x_s, x_r).wait_recv()

        total = f32(glb[pl.ds(mult(x * 2 * rows, 16), 2 * rows), :])
        for s in range(1, x_peers):
            total += f32(x_in[s - 1])
        x_part[...] = total.astype(BF)
        yl_copy().start()

        @pl.when(x < x_peers - 1)
        def _():
            sent = (x_peers - 2) * x_full + x_last
            phase(glb.at[pl.ds(0, sent)], x_s, x_r).wait_send()

        @pl.when(x == x_peers - 1)
        def _():
            phase(x_in, x_s, x_r).wait_send()

    def latent_y():
        yl_copy().wait_recv()
        total = f32(x_part[pl.ds(mult(y_lo * rows, 16), rows), :]) + f32(yl_in[...])
        ctx_part[...] = total.astype(BF)
        for s in range(1, PREV + 1):

            @pl.when(me >= s)
            def _():
                ctx_copy(s).start()

        yl_copy().wait_send()

    def latent_blocks():
        for s in range(1, PREV + 1):

            @pl.when(me + s < n_ctx)
            def _():
                ctx_copy(s).wait_recv()

            @pl.when(me + s >= n_ctx)
            def _():
                ctx_in[s - 1] = jnp.zeros(ctx_in.shape[1:], BF)

        total = f32(ctx_part[:, slot_cols(PREV)])
        for s in range(1, PREV + 1):
            total += f32(ctx_in[s - 1])
        gl_ref[head_rows, :] = total.astype(BF)
        for s in FAR_Z:
            headg_copy(s).start()
        own_rows().start()

    some_heads(0, 1)
    weight_terms(0)
    some_heads(2, 3)
    stage_a(0)
    weight_terms(1)
    latent_terms()
    for copy in head_outputs():
        copy.start()
    stage_a(1)
    stage_b(0)
    stage_b(1)
    stage_c(0)
    stage_c(1)
    latent_x()
    stage_d(0)
    stage_d(1)
    latent_y()
    stage_e(0)
    latent_blocks()
    stage_e(1)

    for s in range(1, PREV + 1):

        @pl.when(me >= s)
        def _():
            ctx_copy(s).wait_send()

    phase(gl_out.at[pl.ds(0, (n_head - 1) * rows)], headg_s, headg_r).wait()
    own_rows().wait()
    for copy in head_outputs():
        copy.wait()
    for p in range(len(PIECES)):
        pairg_copy(p).wait()
        keep_copy(p).wait()


def write_out(attn, gq, gl, gw, attn_out, gq_out, gl_out, gk_out, gv_out, *rest):
    stages, load_sem, store_sem = rest[:5], rest[5], rest[6]
    parts = [(gw.at[k, pl.ds(i * 128, 128)], out.at[pl.ds(i * 128, 128)]) for k, out in ((0, gk_out), (1, gv_out)) for i in range(4)]
    parts += [(gq, gq_out), (gl.at[pl.ds(0, LAT + ROPE)], gl_out), (attn, attn_out)]
    spots = [stages[0].at[pl.ds(i * 128, 128)] for i in range(4)]
    spots += [stages[1].at[pl.ds(i * 128, 128)] for i in range(4)]
    spots += list(stages[2:])
    loads = [
        pltpu.make_async_copy(src, spot, load_sem.at[i])
        for i, ((src, _), spot) in enumerate(zip(parts, spots))
    ]
    stores = [
        pltpu.make_async_copy(spot, dst, store_sem.at[i])
        for i, ((_, dst), spot) in enumerate(zip(parts, spots))
    ]
    for load in loads:
        load.start()
    for load, store in zip(loads, stores):
        load.wait()
        store.start()
    for store in stores:
        store.wait()


def per_device(queries, latent, w_key, w_value, grad_out, segment_ids):
    n_ctx = lax.axis_size("ctx")
    n_head = lax.axis_size("head")
    hbm = pl.BlockSpec(memory_space=pltpu.HBM)
    dma = pltpu.SemaphoreType.DMA
    rows = 80

    def buf(*shape, dtype=BF):
        return pltpu.VMEM(shape, dtype)

    def sems(*shape):
        return [dma(shape), dma(shape)]

    attn_out, grad_queries, grad_latent, grad_w = pl.pallas_call(
        functools.partial(kernel, n_ctx, n_head),
        out_shape=[
            jax.ShapeDtypeStruct((TOK, HEADS * VDIM), BF),
            jax.ShapeDtypeStruct((TOK, HEADS * QK), BF),
            jax.ShapeDtypeStruct((rows * n_head, TOK), BF),
            jax.ShapeDtypeStruct((2, LAT, HEADS * NOPE), BF),
        ],
        in_specs=[hbm] * 6,
        out_specs=[hbm] * 4,
        scratch_shapes=[
            buf(TOK, HEADS * VDIM),
            buf(TOK, HEADS * QK),
            buf(rows * n_head, TOK),
            buf(LAT, HEADS * NOPE),
            buf(TOK, HEADS * QK),
            buf(LAT, 2 * HEADS * NOPE),
            buf(TOK, HEADS * VDIM),
            buf(n_ctx, TOK, dtype=jnp.int32),
            buf(LAT + ROPE, WIN),
            buf(2 * HEADS * NOPE, LAT),
            buf(HEADS, TOK, QK),
            buf(HEADS, QK, TOK),
            buf(HEADS, VDIM, TOK),
            buf(HEADS, QK, WIN),
            buf(HEADS, VDIM, WIN),
            buf(TOK, WIN, dtype=jnp.float32),
            buf(HEADS, TOK, WIN, dtype=jnp.float32),
            buf(HEADS, TOK, WIN, dtype=jnp.float32),
            buf(2 * HEADS * NOPE, WIN),
            buf(ROPE, WIN, dtype=jnp.float32),
            *[buf(2, LAT, wide) for wide in WIDE],
            *[buf(LAT, wide) for wide in WIDE],
            *[buf(LAT, wide) for wide in WIDE],
            *[buf(NZ - 1, a // NZ, wide) for a, wide in zip(A_ROWS, WIDE)],
            *[buf(NY, a // NZ, wide) for a, wide in zip(A_ROWS, WIDE)],
            *[buf(NY - 1, max(b // NY, 16), wide) for b, wide in zip(B_ROWS, WIDE)],
            *[buf(NZ - 1, 16, max(wide // 2, 128)) for wide in WIDE],
            *[buf(max(b // NY, 16), wide) for b, wide in zip(B_ROWS, WIDE)],
            buf(rows * n_head, WIN),
            buf(n_head // 2 - 1, 2 * rows, WIN),
            buf(2 * rows, WIN),
            buf(rows, WIN),
            buf(rows, WIN),
            buf(PREV, rows, TOK),
            dma((4 + 2 * len(PIECES),)),
            *sems(2),
            dma,
            dma,
            *sems(2),
            *sems(len(PIECES)),
            *sems(len(PIECES)),
            *sems(len(PIECES)),
            *sems(len(PIECES)),
            *sems(len(PIECES)),
            *sems(len(PIECES)),
            *sems(len(PIECES)),
            *sems(len(PIECES)),
            *sems(len(PIECES)),
            dma,
            dma,
            dma,
            dma,
            *sems(PREV),
            dma,
            dma,
            dma((len(PIECES) + 3,)),
        ],
        compiler_params=pltpu.CompilerParams(
            collective_id=0, has_side_effects=True, vmem_limit_bytes=60 * 2**20
        ),
        name="attention",
    )(queries, latent.T, w_key, w_value, grad_out, segment_ids.reshape(n_ctx, TOK))
    any_space = pl.BlockSpec(memory_space=pl.ANY)
    attn_out, grad_queries, grad_latent, grad_w_key, grad_w_value = pl.pallas_call(
        write_out,
        out_shape=[
            jax.ShapeDtypeStruct((TOK, HEADS * VDIM), BF),
            jax.ShapeDtypeStruct((TOK, HEADS * QK), BF),
            jax.ShapeDtypeStruct((LAT + ROPE, TOK), BF),
            jax.ShapeDtypeStruct((LAT, HEADS * NOPE), BF),
            jax.ShapeDtypeStruct((LAT, HEADS * NOPE), BF),
        ],
        in_specs=[any_space] * 4,
        out_specs=[hbm] * 5,
        scratch_shapes=[
            buf(LAT, HEADS * NOPE),
            buf(LAT, HEADS * NOPE),
            buf(TOK, HEADS * QK),
            buf(LAT + ROPE, TOK),
            buf(TOK, HEADS * VDIM),
            *sems(11),
        ],
        compiler_params=pltpu.CompilerParams(vmem_limit_bytes=60 * 2**20),
        name="write_out",
    )(attn_out, grad_queries, grad_latent, grad_w)
    return (attn_out, grad_queries, grad_latent.T, grad_w_key, grad_w_value)


def solution(mesh):
    return jax.shard_map(
        per_device,
        mesh=mesh,
        in_specs=(
            P("ctx", "head"),
            P("ctx", None),
            P(None, "head"),
            P(None, "head"),
            P("ctx", "head"),
            P(),
        ),
        out_specs=(
            P("ctx", "head"),
            P("ctx", "head"),
            P("ctx", None),
            P(None, "head"),
            P(None, "head"),
        ),
        check_vma=False,
    )
```
